256 devices in a mesh: member: 8 (over y, x_hi), domain: 32 (over z, x_lo, core).
Axes of the slice: x: 4 (x_hi: 2, x_lo: 2; x = x_hi * 2 + x_lo), y: 4, z: 8, core: 2. Of those that a mesh axis runs over, the one named last changes fastest.
Arguments:
- tracer: float32 [64, 3, 512, 1024], P('member', None, 'domain'), may hold values from -6 to 6
- east_speed: float32 [64, 512, 1024], P('member', 'domain'), may hold values from -0.35 to 0.35
- north_speed: float32 [64, 512, 1024], P('member', 'domain'), may hold values from -0.35 to 0.35
- diffusivity: float32 [64], replicated, may hold values from 0.02 to 0.07
- obs_cell: int32 [2, 64, 3], replicated, may hold values from 0 to 1023, as said below
- tile_offset: int32 [2, 64, 2], replicated, may hold values from 0 to 960, as said below
- obs_value: float32 [2, 64], replicated, may hold values from -6 to 6
- obs_error: float32 [2, 64], replicated, may hold values from 0.2 to 1
Outputs:
- analysis: float32 [64, 3, 512, 1024], P(None, None, 'domain', 'member')
The draws below stay inside these ranges and needn't reach their ends.
Inputs may be any that keep to these rules, and one draw needn't show every extreme that they name: `obs_cell`: each row is (level, first index, second index) of a grid cell: level below 3, first index below 512, second below 1024. `tile_offset`: each observation's tile of 32 x 64 cells lies inside the grid and contains the observation's cell.
All inputs are finite; a program needn't handle non-finite values.
Results may differ from the reference program's by a relative error of at most 0.0001.
Values sent between devices are 32-bit elements; how exact they have to be, the bound alone decides.
No kernel may reach another device: no remote copies, remote signals or barrier semaphores. Data moves between devices by JAX's collectives and lax.ppermute only.
A program may use at most 128 MiB of HBM per device.

```python
import math
import jax
import jax.numpy as jnp
from jax import lax

MEMBERS = 64
STRATA_COUNT = 3
NX = 512
NY = 1024
TILE_X = 32
TILE_Y = 64
NOBS = 64
NBATCH = 2


def obs_layout(key):
    key_level = jax.random.fold_in(key, 11)
    key_col = jax.random.fold_in(key, 12)
    key_row = jax.random.fold_in(key, 13)
    key_back_col = jax.random.fold_in(key, 14)
    key_back_row = jax.random.fold_in(key, 15)
    shape_obs = (NBATCH, NOBS)
    obs_level = jax.random.randint(key_level, shape_obs, 0, STRATA_COUNT)
    obs_col = jax.random.randint(key_col, shape_obs, 0, NX)
    obs_row = jax.random.randint(key_row, shape_obs, 0, NY)
    back_col = jax.random.randint(key_back_col, shape_obs, 0, TILE_X)
    back_row = jax.random.randint(key_back_row, shape_obs, 0, TILE_Y)
    obs_level = obs_level.at[0, 0].set(STRATA_COUNT - 1).at[0, 1].set(0)
    obs_col = obs_col.at[0, 0].set(NX - 1).at[0, 1].set(0)
    obs_row = obs_row.at[0, 0].set(NY - 1).at[0, 1].set(0)
    back_col = back_col.at[0, 1].set(0)
    back_row = back_row.at[0, 1].set(0)
    start_col = jnp.clip(obs_col - back_col, 0, NX - TILE_X)
    start_row = jnp.clip(obs_row - back_row, 0, NY - TILE_Y)
    cells = jnp.stack([obs_level, obs_col, obs_row], axis=-1).astype(jnp.int32)
    tiles = jnp.stack([start_col, start_row], axis=-1).astype(jnp.int32)
    return (cells, tiles)


def draw_obs_cell(key, part):
    cells, tiles = obs_layout(key)
    return cells


def draw_tile_offset(key, part):
    cells, tiles = obs_layout(key)
    return tiles


def block_scale(own_key, shape, shards, low, high):
    loudness = 1.0
    for axis_at, blocks in shards:
        steps = jax.random.uniform(jax.random.fold_in(jax.random.fold_in(own_key, 6), axis_at), (blocks,), jnp.float32, low / len(shards), high / len(shards))
        loudness = loudness * jnp.repeat(jnp.exp(steps), shape[axis_at] // blocks).reshape((-1,) + (1,) * (len(shape) - 1 - axis_at))
    return loudness


def normal_values(stream_key, dims, width, bound, pieces=(), kind=jnp.bfloat16):
    entries = width * jax.random.normal(stream_key, dims, jnp.float32)
    if pieces:
        entries = entries * block_scale(stream_key, dims, pieces, -0.22, 0.18)
    return jnp.clip(entries, -bound, bound).astype(kind)


def setup_inputs(seed: int = 0) -> dict:
    keys = jax.random.split(jax.random.key(seed), 9)
    tracer = normal_values(keys[0], (MEMBERS, STRATA_COUNT, NX, NY), 1.0, 6.0, ((0, 8), (2, 32)), jnp.float32)
    east_speed = jnp.clip(jax.random.uniform(keys[1], (MEMBERS, NX, NY), jnp.float32, -0.35, 0.35) * block_scale(keys[1], (MEMBERS, NX, NY), ((0, 8), (1, 32)), -0.4, 0.0), -0.35, 0.35)
    north_speed = jnp.clip(jax.random.uniform(keys[2], (MEMBERS, NX, NY), jnp.float32, -0.35, 0.35) * block_scale(keys[2], (MEMBERS, NX, NY), ((0, 8), (1, 32)), -0.4, 0.0), -0.35, 0.35)
    diffusivity = jnp.clip(jnp.exp(jax.random.uniform(keys[3], (MEMBERS,), jnp.float32, math.log(0.02), math.log(0.07))), 0.02, 0.07)
    obs_cell = draw_obs_cell(jax.random.fold_in(keys[8], 71), 0)
    tile_offset = draw_tile_offset(jax.random.fold_in(keys[8], 71), 0)
    obs_value = normal_values(keys[6], (NBATCH, NOBS), 1.0, 6.0, (), jnp.float32)
    obs_error = jnp.clip(jnp.exp(jax.random.uniform(keys[7], (NBATCH, NOBS), jnp.float32, math.log(0.2), math.log(1.0))), 0.2, 1.0)
    return dict(tracer=tracer, east_speed=east_speed, north_speed=north_speed, diffusivity=diffusivity, obs_cell=obs_cell, tile_offset=tile_offset, obs_value=obs_value, obs_error=obs_error)


def concentration_change(halo_padded, depth_levels, diff_rates, wall_mask):
    tracer = halo_padded[:, :depth_levels]
    east_vel = halo_padded[:, depth_levels]
    north_vel = halo_padded[:, depth_levels + 1]
    rate_col = diff_rates[:, None, None, None]
    east_face = 0.5 * (east_vel[:, :-1, 1:-1] + east_vel[:, 1:, 1:-1])
    behind = tracer[:, :, :-1, 1:-1]
    ahead_cells = tracer[:, :, 1:, 1:-1]
    flux_east = jnp.maximum(east_face, 0.0)[:, None] * behind + jnp.minimum(east_face, 0.0)[:, None] * ahead_cells - rate_col * (ahead_cells - behind)
    north_face = 0.5 * (north_vel[:, 1:-1, :-1] + north_vel[:, 1:-1, 1:])
    lower_cells = tracer[:, :, 1:-1, :-1]
    upper_cells = tracer[:, :, 1:-1, 1:]
    flux_north = (jnp.maximum(north_face, 0.0)[:, None] * lower_cells + jnp.minimum(north_face, 0.0)[:, None] * upper_cells - rate_col * (upper_cells - lower_cells)) * wall_mask
    centre = tracer[:, :, 1:-1, 1:-1]
    return centre - (flux_east[:, :, 1:] - flux_east[:, :, :-1]) - (flux_north[..., 1:] - flux_north[..., :-1])

def taper(position, centre, first_cell, tile_span):
    inside = (position >= first_cell) & (position < first_cell + tile_span)
    return jnp.where(inside, 1.0 - jnp.abs(position - centre).astype(jnp.float32) / tile_span, 0.0)

def localize(level_ids, col_ids, row_ids, obs_level, obs_col, obs_row, start_col, start_row):
    vertical = jnp.where(level_ids == obs_level, 1.0, 0.5)
    across = taper(col_ids, obs_col, start_col, TILE_X)
    along = taper(row_ids, obs_row, start_row, TILE_Y)
    return vertical[:, None, None] * across[None, :, None] * along[None, None, :]

def innovation(priors, obs_index, obs_values, obs_errors):
    members = priors.shape[1]
    current = priors[obs_index]
    average = jnp.mean(current)
    spread = current - average
    variance = jnp.sum(spread * spread) / (members - 1)
    measurement_noise = obs_errors[obs_index]
    divisor_term = variance + measurement_noise
    reduction = 1.0 / (1.0 + jnp.sqrt(measurement_noise / divisor_term))
    correction = obs_values[obs_index] - average - reduction * spread
    factor = 1.0 / ((members - 1) * divisor_term)
    return (spread, correction, factor)

def update_priors(priors, spread, correction, factor, obs_cells, obs_level, obs_col, obs_row, start_col, start_row):
    obs_cov = jnp.dot(priors, spread, precision=lax.Precision.HIGHEST)
    obs_weight = jnp.where(obs_cells[:, 0] == obs_level, 1.0, 0.5) * taper(obs_cells[:, 1], obs_col, start_col, TILE_X) * taper(obs_cells[:, 2], obs_row, start_row, TILE_Y)
    return priors + (obs_weight * obs_cov * factor)[:, None] * correction[None, :]

def reference_batch(ensemble_fields, priors, obs_cells, obs_tiles, obs_values, obs_errors):
    members = ensemble_fields.shape[0]
    depth_levels = ensemble_fields.shape[1]
    level_ids = jnp.arange(depth_levels)
    zero_index = jnp.zeros((), jnp.int32)

    def serial_step(obs_index, carried):
        ensemble_fields, priors = carried
        spread, correction, factor = innovation(priors, obs_index, obs_values, obs_errors)
        obs_level = obs_cells[obs_index, 0]
        obs_col = obs_cells[obs_index, 1]
        obs_row = obs_cells[obs_index, 2]
        start_col = obs_tiles[obs_index, 0].astype(jnp.int32)
        start_row = obs_tiles[obs_index, 1].astype(jnp.int32)
        window = lax.dynamic_slice(ensemble_fields, (zero_index, zero_index, start_col, start_row), (members, depth_levels, TILE_X, TILE_Y))
        col_ids = start_col + jnp.arange(TILE_X, dtype=jnp.int32)
        row_ids = start_row + jnp.arange(TILE_Y, dtype=jnp.int32)
        weight = localize(level_ids, col_ids, row_ids, obs_level, obs_col, obs_row, start_col, start_row)
        covariance = jnp.einsum('mlxy,m->lxy', window, spread, precision=lax.Precision.HIGHEST)
        window = window + (weight * covariance * factor)[None] * correction[:, None, None, None]
        ensemble_fields = lax.dynamic_update_slice(ensemble_fields, window, (zero_index, zero_index, start_col, start_row))
        priors = update_priors(priors, spread, correction, factor, obs_cells, obs_level, obs_col, obs_row, start_col, start_row)
        return (ensemble_fields, priors)
    return lax.fori_loop(0, obs_cells.shape[0], serial_step, (ensemble_fields, priors))

def reference(tracer, east_speed, north_speed, diffusivity, obs_cell, tile_offset, obs_value, obs_error):
    depth_levels = tracer.shape[1]
    stacked = jnp.concatenate([tracer, east_speed[:, None], north_speed[:, None]], axis=1)
    halo_padded = jnp.pad(stacked, ((0, 0), (0, 0), (1, 1), (0, 0)), mode='wrap')
    halo_padded = jnp.pad(halo_padded, ((0, 0), (0, 0), (0, 0), (1, 1)))
    face_ids = jnp.arange(NY + 1)
    wall_mask = jnp.where((face_ids == 0) | (face_ids == NY), 0.0, 1.0)

    def one_member(member_pair):
        member_block, member_rate = member_pair
        return concentration_change(member_block[None], depth_levels, member_rate[None], wall_mask)[0]
    ensemble_fields = lax.map(one_member, (halo_padded, diffusivity))
    for batch_num in range(NBATCH):
        obs_cells = obs_cell[batch_num]
        priors = ensemble_fields[:, obs_cells[:, 0], obs_cells[:, 1], obs_cells[:, 2]].T
        ensemble_fields, priors = reference_batch(ensemble_fields, priors, obs_cells, tile_offset[batch_num], obs_value[batch_num], obs_error[batch_num])
    return ensemble_fields
```

```python
import functools

import jax
import jax.numpy as jnp
from jax import lax
from jax.experimental import pallas as pl
from jax.experimental.pallas import tpu as pltpu
from jax.sharding import PartitionSpec as P

TILE_X = 32
TILE_Y = 64
LANES = 128
NONE = 999.0
LAST = 0x7FFFFFFF
PLANES = 5
VMEM_BYTES = 32 * 1024 * 1024
WHOLE_VMEM = 64 * 1024 * 1024 - 65536


def lane_row(ref, *index):
    return jnp.concatenate([ref[(*index, slice(0, 1))], ref[(*index, slice(1, 2))]], axis=1)


def copies(pairs, sems):
    made = [pltpu.make_async_copy(src, dst, sems.at[i]) for i, (src, dst) in enumerate(pairs)]
    for one in made:
        one.start()
    return made


def face_flux(u_low, u_high, q_low, q_high, rate):
    face = 0.5 * (u_low + u_high)
    return (
        jnp.maximum(face, 0.0) * q_low + jnp.minimum(face, 0.0) * q_high - rate * (q_high - q_low)
    )


def prepare_kernel(
    domains, cell_ref, tile_ref, rate_ref, tracer_hbm, east_hbm, north_hbm,
    low_ref, high_ref, picked_ref, meta_ref, tracer_ref, east_ref, north_ref, sems,
):
    members, levels, cols, length = tracer_ref.shape
    loads = copies(
        [(tracer_hbm, tracer_ref), (east_hbm, east_ref), (north_hbm, north_ref)], sems
    )
    domain = lax.axis_index("domain")
    me = lax.axis_index("member")
    col0 = domain * cols
    width = domains * cols
    level = lane_row(cell_ref, 0)
    x = lane_row(cell_ref, 1)
    y = lane_row(cell_ref, 2)
    ox = jnp.concatenate([tile_ref[0, 0:1], tile_ref[1, 0:1]], axis=1)
    oy = jnp.concatenate([tile_ref[0, 1:2], tile_ref[1, 1:2]], axis=1)
    lane = lax.broadcasted_iota(jnp.int32, (1, LANES), 1)
    zero = jnp.zeros((3, LANES), jnp.int32)
    meta_ref[...] = jnp.concatenate([level, x, y, ox, oy, zero], axis=0)
    near = (x >= col0) & (x < col0 + cols)
    before = jnp.where(col0 == 0, width, col0) - 1
    after = jnp.where(col0 + cols == width, 0, col0 + cols)
    near = near | (x == before) | (x == after)
    keys = jnp.where(near, (lane << 21) + (level << 19) + (x << 10) + y, LAST)
    picked_ref[...] = jnp.zeros_like(picked_ref)
    for one in loads:
        one.wait()
    for i, edge in ((0, low_ref), (cols - 1, high_ref)):
        edge[:, :levels] = tracer_ref[:, :, i]
        edge[:, levels] = east_ref[:, i]

    sub = lax.broadcasted_iota(jnp.int32, (members, LANES), 0)
    lanes = lax.broadcasted_iota(jnp.int32, (members, LANES), 1)
    rates = jnp.zeros((members, LANES), jnp.float32)
    for m in range(members):
        rates = jnp.where(sub == m, rate_ref[me * members + m], rates)

    def pick(key):
        k = key >> 21
        l = (key >> 19) & 3
        col = (key >> 10) & 511
        row = key & 1023
        here = col - col0
        own = (here >= 0) & (here < cols)

        def fetch(ref, lead, i, j):
            i = jnp.clip(i, 0, cols - 1)
            j = jnp.clip(j, 0, length - 1)
            first = pl.multiple_of((i >> 3) << 3, 8)
            start = pl.multiple_of((j >> 7) << 7, LANES)
            rows = jnp.zeros((members, LANES), jnp.float32)
            for m in range(members):
                tile = ref[(m, *lead, pl.ds(first, 8), pl.ds(start, LANES))]
                rows = jnp.where(sub == m, pltpu.roll(tile, (m - i) & 7, 0), rows)
            return pltpu.roll(rows, (k - (j & 127) + LANES) & 127, 1)

        mine = lanes == k

        def put(plane, value):
            at = slice(plane * members, (plane + 1) * members)
            picked_ref[at] = jnp.where(mine, value, picked_ref[at])

        @pl.when(own)
        def _():
            q = fetch(tracer_ref, (l,), here, row)
            u = fetch(east_ref, (), here, row)
            v = fetch(north_ref, (), here, row)
            south = face_flux(
                fetch(north_ref, (), here, row - 1), v, fetch(tracer_ref, (l,), here, row - 1), q, rates
            )
            north = face_flux(
                v, fetch(north_ref, (), here, row + 1), q, fetch(tracer_ref, (l,), here, row + 1), rates
            )
            low = face_flux(
                fetch(east_ref, (), here - 1, row), u, fetch(tracer_ref, (l,), here - 1, row), q, rates
            )
            high = face_flux(
                u, fetch(east_ref, (), here + 1, row), q, fetch(tracer_ref, (l,), here + 1, row), rates
            )
            south = jnp.where(row == 0, 0.0, south)
            north = jnp.where(row == length - 1, 0.0, north)
            low = jnp.where(here == 0, 0.0, low)
            high = jnp.where(here == cols - 1, 0.0, high)
            put(0, q - (high - low) - (north - south))
            put(1, q)
            put(2, u)

        @pl.when(jnp.logical_not(own))
        def _():
            there = jnp.where(col == before, 0, cols - 1)
            put(3, fetch(tracer_ref, (l,), there, row))
            put(4, fetch(east_ref, (), there, row))

    def step(key):
        pick(key)
        return jnp.min(jnp.where(keys > key, keys, LAST))

    lax.while_loop(lambda key: key < LAST, step, jnp.min(keys))


def prepare(cells, tiles, rates, tracer, east, north, domains):
    members, levels, cols, length = tracer.shape
    vmem = pl.BlockSpec(memory_space=pltpu.VMEM)
    hbm = pl.BlockSpec(memory_space=pltpu.HBM)
    edge = jax.ShapeDtypeStruct((members, levels + 1, length), jnp.float32)
    return pl.pallas_call(
        functools.partial(prepare_kernel, domains),
        out_shape=[
            edge,
            edge,
            jax.ShapeDtypeStruct((PLANES * members, LANES), jnp.float32),
            jax.ShapeDtypeStruct((8, LANES), jnp.int32),
        ],
        in_specs=[vmem, vmem, pl.BlockSpec(memory_space=pltpu.SMEM), hbm, hbm, hbm],
        out_specs=[vmem] * 4,
        scratch_shapes=[
            pltpu.VMEM(tracer.shape, jnp.float32),
            pltpu.VMEM(east.shape, jnp.float32),
            pltpu.VMEM(north.shape, jnp.float32),
            pltpu.SemaphoreType.DMA((3,)),
        ],
        compiler_params=pltpu.CompilerParams(vmem_limit_bytes=WHOLE_VMEM),
        cost_estimate=pl.CostEstimate(flops=1_000_000, bytes_accessed=3_000_000, transcendentals=0),
        name="prepare",
    )(cells, tiles, rates, tracer, east, north)


def forecast_kernel(
    rate_ref, below_ref, above_ref, tracer_ref, east_ref, north_ref, out_ref
):
    members, levels, cols, length = tracer_ref.shape
    bands = out_ref.shape[0]
    me = lax.axis_index("member")
    lane = lax.broadcasted_iota(jnp.int32, (cols, LANES), 1)

    def sides(read, d):
        here = read(d)
        left = jnp.where(lane == LANES - 1, read(d - 1), here) if d else here
        right = jnp.where(lane == 0, read(d + 1), here) if d < bands - 1 else here
        return (pltpu.roll(left, 1, 1), here, pltpu.roll(right, LANES - 1, 1))

    def weights(low, high, rate):
        face = 0.5 * (low + high)
        return (jnp.maximum(face, 0.0) + rate, jnp.minimum(face, 0.0) - rate)

    def member(g, carry):
        rate = rate_ref[me * members + g]
        for d in range(bands):
            at = lambda i: pl.ds(i * LANES, LANES)
            u = east_ref[g, :, at(d)]
            u_low = jnp.concatenate([below_ref[g, levels : levels + 1, at(d)], u[:-1]], axis=0)
            behind, ahead = weights(u_low, u, rate)
            behind_last, ahead_last = weights(
                u[-1:], above_ref[g, levels : levels + 1, at(d)], rate
            )
            v_left, v, v_right = sides(lambda i: north_ref[g, :, at(i)], d)
            south_low, south_high = weights(v_left, v, rate)
            north_low, north_high = weights(v, v_right, rate)
            if d == 0:
                south_low = jnp.where(lane == 0, 0.0, south_low)
                south_high = jnp.where(lane == 0, 0.0, south_high)
            if d == bands - 1:
                north_low = jnp.where(lane == LANES - 1, 0.0, north_low)
                north_high = jnp.where(lane == LANES - 1, 0.0, north_high)
            for l in range(levels):
                q_left, q, q_right = sides(lambda i: tracer_ref[g, l, :, at(i)], d)
                q_low = jnp.concatenate([below_ref[g, l : l + 1, at(d)], q[:-1]], axis=0)
                flux = behind * q_low + ahead * q
                flux_last = behind_last * q[-1:] + ahead_last * above_ref[g, l : l + 1, at(d)]
                flux_up = jnp.concatenate([flux[1:], flux_last], axis=0)
                south = south_low * q_left + south_high * q
                north = north_low * q + north_high * q_right
                out_ref[d, g, l] = q - (flux_up - flux) - (north - south)
        return carry

    lax.fori_loop(0, members, member, 0)


def forecast(rates, below, above, tracer, east, north, bands):
    members, levels, cols, length = tracer.shape
    vmem = pl.BlockSpec(memory_space=pltpu.VMEM)
    return pl.pallas_call(
        forecast_kernel,
        out_shape=jax.ShapeDtypeStruct((bands, members, levels, cols, LANES), jnp.float32),
        in_specs=[pl.BlockSpec(memory_space=pltpu.SMEM)] + [vmem] * 5,
        out_specs=vmem,
        compiler_params=pltpu.CompilerParams(vmem_limit_bytes=VMEM_BYTES),
        cost_estimate=pl.CostEstimate(
            flops=16_000_000, bytes_accessed=4_500_000, transcendentals=0
        ),
        name="forecast",
    )(rates, below, above, tracer, east, north)


def innovations(priors, values, errors):
    members = priors.shape[0]
    average = jnp.sum(priors, axis=0, keepdims=True) / members
    spread = priors - average
    variance = jnp.sum(spread * spread, axis=0, keepdims=True) / (members - 1)
    divisor = variance + errors
    reduction = 1.0 / (1.0 + jnp.sqrt(errors / divisor))
    factor = 1.0 / ((members - 1) * divisor)
    return (spread, values - average, reduction, factor)


def solve_kernel(prior_ref, meta_ref, value_ref, error_ref, out_ref):
    members, total = prior_ref.shape
    meta = meta_ref[...].astype(jnp.float32)
    across = jnp.concatenate(
        [meta, jnp.zeros((total - meta.shape[0], total), jnp.float32)], axis=0
    ).T
    level_j, x_j, y_j, ox_j, oy_j = (across[:, i : i + 1] for i in range(5))
    level_k, x_k, y_k = (meta[i : i + 1] for i in range(3))
    j_ids = lax.broadcasted_iota(jnp.int32, (total, total), 0)
    k_ids = lax.broadcasted_iota(jnp.int32, (total, total), 1)
    source = j_ids.astype(jnp.float32)
    taper_x = jnp.where(
        (x_k >= ox_j) & (x_k < ox_j + TILE_X), 1.0 - jnp.abs(x_k - x_j) / TILE_X, 0.0
    )
    taper_y = jnp.where(
        (y_k >= oy_j) & (y_k < oy_j + TILE_Y), 1.0 - jnp.abs(y_k - y_j) / TILE_Y, 0.0
    )
    weight = jnp.where(level_j == level_k, 1.0, 0.5) * taper_x * taper_y
    weight = jnp.where(j_ids < k_ids, weight, 0.0)
    pending = jnp.where(weight != 0.0, source, -1.0)
    values = lane_row(value_ref)
    errors = lane_row(error_ref)

    def following(done):
        return jnp.min(jnp.where(pending > done, pending, NONE), axis=0, keepdims=True)

    def step(carry):
        priors, nxt, left = carry
        spread, offset, reduction, factor = innovations(priors, values, errors)
        final = jnp.where(nxt == NONE, 1.0, 0.0)
        table = jnp.concatenate(
            [spread, offset, reduction, factor, final, jnp.zeros((12, total), jnp.float32)], axis=0
        )
        high = table.astype(jnp.bfloat16)
        rest = table - high.astype(jnp.float32)
        middle = rest.astype(jnp.bfloat16)
        low = (rest - middle.astype(jnp.float32)).astype(jnp.bfloat16)
        chosen = source == nxt
        pick = jnp.where(chosen, 1.0, 0.0).astype(jnp.bfloat16)
        dot = lambda part: jnp.dot(part, pick, preferred_element_type=jnp.float32)
        got = dot(high) + dot(middle) + dot(low)
        their_spread = got[:members]
        their_offset, their_reduction, their_factor, ready = (
            got[members + i : members + i + 1] for i in range(4)
        )
        rho = jnp.sum(jnp.where(chosen, weight, 0.0), axis=0, keepdims=True)
        covariance = jnp.sum(priors * their_spread, axis=0, keepdims=True)
        go = ready > 0.5
        scale = jnp.where(go, rho * covariance * their_factor, 0.0)
        priors = priors + scale * (their_offset - their_reduction * their_spread)
        done = jnp.where(go, nxt, nxt - 0.5)
        nxt = following(done)
        return (priors, nxt, jnp.min(nxt))

    nxt = following(jnp.full((1, total), -1.0, jnp.float32))
    priors, _, _ = lax.while_loop(
        lambda carry: carry[2] < NONE, step, (prior_ref[...], nxt, jnp.min(nxt))
    )
    spread, offset, reduction, factor = innovations(priors, values, errors)
    out_ref[0] = spread * factor
    out_ref[1] = offset - reduction * spread


def solve_filter(priors, meta, values, errors):
    vmem = pl.BlockSpec(memory_space=pltpu.VMEM)
    return pl.pallas_call(
        solve_kernel,
        out_shape=jax.ShapeDtypeStruct((2, *priors.shape), jnp.float32),
        in_specs=[vmem] * 4,
        out_specs=vmem,
        name="solve_filter",
    )(priors, meta, values, errors)


def apply_kernel(
    local_members, meta_ref, lanes_ref, table_ref, in_ref, out_ref, work, gain, sems_in, sems_out
):
    members, levels, cols, rows = work.shape
    part = 8
    parts = cols // part
    loads = copies(
        [
            (in_ref.at[:, l, pl.ds(g * part, part)], work.at[:, l, pl.ds(g * part, part)])
            for g in range(parts)
            for l in range(levels)
        ],
        sems_in,
    )
    me = lax.axis_index("member")
    base = lax.axis_index("domain") * cols
    row0 = me * rows
    lane = lax.broadcasted_iota(jnp.int32, (1, LANES), 1)
    ox = lanes_ref[3:4]
    oy = lanes_ref[4:5]
    in_rows = (oy < row0 + rows) & (oy + TILE_Y > row0)

    def taper(position, centre, first, span):
        inside = (position >= first) & (position < first + span)
        return jnp.where(inside, 1.0 - jnp.abs(position - centre).astype(jnp.float32) / span, 0.0)

    def member_row(m):
        return ((m // local_members) ^ me) * local_members + m % local_members

    stores = []
    for g in range(parts):
        for one in loads[g * levels : (g + 1) * levels]:
            one.wait()
        col0 = base + g * part
        keys = jnp.where(in_rows & (ox < col0 + part) & (ox + TILE_X > col0), lane, LAST)
        col_ids = col0 + lax.broadcasted_iota(jnp.int32, (part, rows), 0)
        row_ids = row0 + lax.broadcasted_iota(jnp.int32, (part, rows), 1)
        band = pl.ds(g * part, part)

        def update(k, keys=keys, col_ids=col_ids, row_ids=row_ids, band=band):
            shift = (LANES - k) & 127
            for i in range(2):
                column = pltpu.roll(table_ref[i], shift, 1)[:, 0:1]
                gain[i] = jnp.broadcast_to(column, (members, LANES))
            weight = taper(col_ids, meta_ref[1, k], meta_ref[3, k], TILE_X) * taper(
                row_ids, meta_ref[2, k], meta_ref[4, k], TILE_Y
            )
            sums = [[None, None] for _ in range(levels)]
            for m in range(members):
                s = gain[0, pl.ds(member_row(m), 1)]
                for l in range(levels):
                    term = work[m, l, band] * s
                    old = sums[l][m % 2]
                    sums[l][m % 2] = term if old is None else old + term
            scale = []
            for l in range(levels):
                vertical = jnp.where(meta_ref[0, k] == l, 1.0, 0.5)
                scale.append(vertical * weight * (sums[l][0] + sums[l][1]))
            for m in range(members):
                c = gain[1, pl.ds(member_row(m), 1)]
                for l in range(levels):
                    work[m, l, band] = work[m, l, band] + scale[l] * c
            return jnp.min(jnp.where(keys > k, keys, LAST))

        lax.while_loop(lambda k: k < LAST, update, jnp.min(keys))
        for l in range(levels):
            one = pltpu.make_async_copy(
                work.at[:, l, band], out_ref.at[:, l, band], sems_out.at[g * levels + l]
            )
            one.start()
            stores.append(one)
    for one in stores:
        one.wait()


def apply_updates(meta, table, block, local_members):
    members, levels, cols, rows = block.shape
    vmem = pl.BlockSpec(memory_space=pltpu.VMEM)
    some = pl.BlockSpec(memory_space=pl.ANY)
    count = levels * cols // 8
    return pl.pallas_call(
        functools.partial(apply_kernel, local_members),
        out_shape=jax.ShapeDtypeStruct(block.shape, jnp.float32),
        in_specs=[pl.BlockSpec(memory_space=pltpu.SMEM), vmem, vmem, some],
        out_specs=some,
        scratch_shapes=[
            pltpu.VMEM(block.shape, jnp.float32),
            pltpu.VMEM((2, members, LANES), jnp.float32),
            pltpu.SemaphoreType.DMA((count,)),
            pltpu.SemaphoreType.DMA((count,)),
        ],
        compiler_params=pltpu.CompilerParams(vmem_limit_bytes=WHOLE_VMEM),
        name="apply_updates",
    )(meta, meta, table, block)


def exchange(array, axis, peers, reach):
    return lax.ppermute(array, axis, [(i, i ^ reach) for i in range(peers)])


def finish_priors(picked, meta, rates, cols):
    whole, q, u, q_far, u_far = jnp.split(picked, PLANES, axis=0)
    place = meta[1:2] & (cols - 1)
    rate = rates[:, None]
    low = face_flux(u_far, u, q_far, q, rate)
    high = face_flux(u, u_far, q, q_far, rate)
    return whole + jnp.where(place == 0, low, 0.0) - jnp.where(place == cols - 1, high, 0.0)


def local(
    tracer, east_speed, north_speed, diffusivity, obs_cell, tile_offset, obs_value, obs_error
):
    members, levels, cols, length = tracer.shape
    bands = lax.axis_size("member")
    domains = lax.axis_size("domain")
    cells = obs_cell.transpose(2, 0, 1)
    tiles = tile_offset.transpose(0, 2, 1)
    rates = lax.dynamic_slice_in_dim(diffusivity, lax.axis_index("member") * members, members)
    low, high, picked, meta = prepare(
        cells, tiles, diffusivity, tracer, east_speed, north_speed, domains
    )
    up = [(i, (i + 1) % domains) for i in range(domains)]
    down = [(j, i) for i, j in up]
    below = lax.ppermute(high, "domain", up)
    above = lax.ppermute(low, "domain", down)
    for reach in (1, 2):
        picked = picked + exchange(picked, "domain", domains, reach)
    below, above, picked = lax.optimization_barrier((below, above, picked))
    blocks = forecast(diffusivity, below, above, tracer, east_speed, north_speed, bands)
    picked = picked + exchange(picked, "domain", domains, 4)
    blocks, picked = lax.optimization_barrier((blocks, picked))
    block = lax.all_to_all(blocks, "member", split_axis=0, concat_axis=0, tiled=True)
    block = block.reshape(bands * members, levels, cols, length // bands)
    reach = 8
    while reach < domains:
        picked = picked + exchange(picked, "domain", domains, reach)
        reach *= 2
    priors = finish_priors(picked, meta, rates, cols)
    reach = 1
    while reach < bands:
        priors = jnp.concatenate([priors, exchange(priors, "member", bands, reach)], axis=0)
        reach *= 2
    table = solve_filter(priors, meta, obs_value, obs_error)
    return apply_updates(meta, table, block, members)


def solution(mesh):
    placed = (
        P("member", None, "domain", None),
        P("member", "domain", None),
        P("member", "domain", None),
        P(),
        P(),
        P(),
        P(),
        P(),
    )
    return jax.shard_map(
        local,
        mesh=mesh,
        in_specs=placed,
        out_specs=P(None, None, "domain", "member"),
        check_vma=False,
    )
```

```python
import functools

import jax
import jax.numpy as jnp
from jax import lax
from jax.experimental import pallas as pl
from jax.experimental.pallas import tpu as pltpu
from jax.sharding import PartitionSpec as P

TILE_X = 32
TILE_Y = 64
LANES = 128
NONE = 999.0
LAST = 0x7FFFFFFF
PLANES = 5
STEPS = (4, 6)
VMEM_BYTES = 32 * 1024 * 1024


def lane_row(ref, *index):
    return jnp.concatenate([ref[(*index, slice(0, 1))], ref[(*index, slice(1, 2))]], axis=1)


def copies(pairs, sems):
    made = [pltpu.make_async_copy(src, dst, sems.at[i]) for i, (src, dst) in enumerate(pairs)]
    for one in made:
        one.start()
    return made


def face_flux(u_low, u_high, q_low, q_high, rate):
    face = 0.5 * (u_low + u_high)
    return (
        jnp.maximum(face, 0.0) * q_low + jnp.minimum(face, 0.0) * q_high - rate * (q_high - q_low)
    )


def prepare_kernel(
    domains, cell_hbm, tile_hbm, rate_hbm, tracer_hbm, east_hbm, north_hbm,
    inner_ref, outer_ref, meta_ref, tracer_ref, east_ref, north_ref,
    cell_ref, tile_ref, rate_ref, sems,
):
    members, levels, cols, length = tracer_ref.shape
    bands = length // LANES
    small = copies(
        [(cell_hbm, cell_ref), (tile_hbm, tile_ref), (rate_hbm, rate_ref)], sems.at[0]
    )
    loads = copies(
        [(tracer_hbm, tracer_ref), (east_hbm, east_ref), (north_hbm, north_ref)], sems.at[1]
    )
    for one in small:
        one.wait()
    domain = lax.axis_index("domain")
    me = lax.axis_index("member")
    col0 = domain * cols
    width = domains * cols
    level = lane_row(cell_ref, 0)
    x = lane_row(cell_ref, 1)
    y = lane_row(cell_ref, 2)
    ox = jnp.concatenate([tile_ref[0, 0:1], tile_ref[1, 0:1]], axis=1)
    oy = jnp.concatenate([tile_ref[0, 1:2], tile_ref[1, 1:2]], axis=1)
    lane = lax.broadcasted_iota(jnp.int32, (1, LANES), 1)
    zero = jnp.zeros((3, LANES), jnp.int32)
    meta_ref[...] = jnp.concatenate([level, x, y, ox, oy, zero], axis=0)
    near = (x >= col0) & (x < col0 + cols)
    before = jnp.where(col0 == 0, width, col0) - 1
    after = jnp.where(col0 + cols == width, 0, col0 + cols)
    near = near | (x == before) | (x == after)
    keys = jnp.where(near, (lane << 21) + (level << 19) + (x << 10) + y, LAST)
    for one in loads:
        one.wait()
    first_core = (domain & 1) == 0
    for p in range(levels + 1):
        for d in range(bands):
            at = slice(d * LANES, (d + 1) * LANES)
            plane = tracer_ref.at[:, p] if p < levels else east_ref
            low = plane[:, 0, at]
            high = plane[:, cols - 1, at]
            inner_ref[:, p * bands + d] = jnp.where(first_core, high, low)
            outer_ref[:, p * bands + d] = jnp.where(first_core, low, high)

    sub = lax.broadcasted_iota(jnp.int32, (members, LANES), 0)
    lanes = lax.broadcasted_iota(jnp.int32, (members, LANES), 1)
    rates = jnp.zeros((members, LANES), jnp.float32)
    for m in range(members):
        rates = jnp.where(sub == m, rate_ref[me * members + m], rates)

    def pick(carry):
        key, planes = carry
        following = jnp.min(jnp.where(keys > key, keys, LAST))
        k = key >> 21
        l = (key >> 19) & 3
        col = (key >> 10) & 511
        row = key & 1023
        own = (col >= col0) & (col < col0 + cols)
        here = jnp.where(own, col - col0, jnp.where(col == before, 0, cols - 1))

        def fetch(ref, lead, i, j):
            i = jnp.clip(i, 0, cols - 1)
            j = jnp.clip(j, 0, length - 1)
            first = pl.multiple_of((i >> 3) << 3, 8)
            start = pl.multiple_of((j >> 7) << 7, LANES)
            rows = jnp.zeros((members, LANES), jnp.float32)
            for m in range(members):
                tile = ref[(m, *lead, pl.ds(first, 8), pl.ds(start, LANES))]
                rows = jnp.where(sub == m, pltpu.roll(tile, (m - i) & 7, 0), rows)
            return pltpu.roll(rows, (k - (j & 127) + LANES) & 127, 1)

        q = fetch(tracer_ref, (l,), here, row)
        u = fetch(east_ref, (), here, row)
        v = fetch(north_ref, (), here, row)
        south = face_flux(
            fetch(north_ref, (), here, row - 1), v, fetch(tracer_ref, (l,), here, row - 1), q, rates
        )
        north = face_flux(
            v, fetch(north_ref, (), here, row + 1), q, fetch(tracer_ref, (l,), here, row + 1), rates
        )
        low = face_flux(
            fetch(east_ref, (), here - 1, row), u, fetch(tracer_ref, (l,), here - 1, row), q, rates
        )
        high = face_flux(
            u, fetch(east_ref, (), here + 1, row), q, fetch(tracer_ref, (l,), here + 1, row), rates
        )
        south = jnp.where(row == 0, 0.0, south)
        north = jnp.where(row == length - 1, 0.0, north)
        low = jnp.where(here == 0, 0.0, low)
        high = jnp.where(here == cols - 1, 0.0, high)
        mine = lanes == k
        ours = mine & own
        theirs = mine & jnp.logical_not(own)
        values = (
            (ours, q - (high - low) - (north - south)), (ours, q), (ours, u), (theirs, q), (theirs, u)
        )
        planes = tuple(jnp.where(at, new, old) for (at, new), old in zip(values, planes))
        return (following, planes)

    blank = jnp.zeros((members, LANES), jnp.float32)
    _, planes = lax.while_loop(
        lambda carry: carry[0] < LAST, pick, (jnp.min(keys), (blank,) * PLANES)
    )
    for i, plane in enumerate(planes):
        inner_ref[:, (levels + 1) * bands + i] = plane
    for i in range(PLANES, 8):
        inner_ref[:, (levels + 1) * bands + i] = blank


def in_hbm(*arrays):
    return [pltpu.with_memory_space_constraint(a, pltpu.HBM) for a in arrays]


def prepare(cells, tiles, rates, tracer, east, north, domains):
    members, levels, cols, length = tracer.shape
    vmem = pl.BlockSpec(memory_space=pltpu.VMEM)
    hbm = pl.BlockSpec(memory_space=pltpu.HBM)
    sent = jax.ShapeDtypeStruct(
        (members, (levels + 1) * (length // LANES) + 8, LANES), jnp.float32
    )
    return pl.pallas_call(
        functools.partial(prepare_kernel, domains),
        out_shape=[
            sent,
            sent,
            jax.ShapeDtypeStruct((8, LANES), jnp.int32),
            jax.ShapeDtypeStruct(tracer.shape, jnp.float32),
            jax.ShapeDtypeStruct(east.shape, jnp.float32),
            jax.ShapeDtypeStruct(north.shape, jnp.float32),
        ],
        in_specs=[hbm] * 6,
        out_specs=[vmem] * 6,
        scratch_shapes=[
            pltpu.VMEM(cells.shape, jnp.int32),
            pltpu.VMEM(tiles.shape, jnp.int32),
            pltpu.SMEM(rates.shape, jnp.float32),
            pltpu.SemaphoreType.DMA((2, 3)),
        ],
        compiler_params=pltpu.CompilerParams(vmem_limit_bytes=VMEM_BYTES),
        cost_estimate=pl.CostEstimate(flops=1_000_000, bytes_accessed=3_000_000, transcendentals=0),
        name="prepare",
    )(*in_hbm(cells, tiles, rates, tracer, east, north))


def face_weights(low, high, rate):
    face = 0.5 * (low + high)
    return (jnp.maximum(face, 0.0) + rate, jnp.minimum(face, 0.0) - rate)


def interior_kernel(rate_ref, tracer_ref, east_ref, north_ref, out_ref):
    members, levels, cols, length = tracer_ref.shape
    bands = out_ref.shape[0]
    me = lax.axis_index("member")
    lane = lax.broadcasted_iota(jnp.int32, (cols, LANES), 1)
    none = jnp.zeros((1, LANES), jnp.float32)

    def sides(read, d):
        here = read(d)
        left = jnp.where(lane == LANES - 1, read(d - 1), here) if d else here
        right = jnp.where(lane == 0, read(d + 1), here) if d < bands - 1 else here
        return (pltpu.roll(left, 1, 1), here, pltpu.roll(right, LANES - 1, 1))

    def member(g, carry):
        rate = rate_ref[me * members + g]
        for d in range(bands):
            at = lambda i: pl.ds(i * LANES, LANES)
            u = east_ref[g, :, at(d)]
            behind, ahead = face_weights(u[:-1], u[1:], rate)
            v_left, v, v_right = sides(lambda i: north_ref[g, :, at(i)], d)
            south_low, south_high = face_weights(v_left, v, rate)
            north_low, north_high = face_weights(v, v_right, rate)
            if d == 0:
                south_low = jnp.where(lane == 0, 0.0, south_low)
                south_high = jnp.where(lane == 0, 0.0, south_high)
            if d == bands - 1:
                north_low = jnp.where(lane == LANES - 1, 0.0, north_low)
                north_high = jnp.where(lane == LANES - 1, 0.0, north_high)
            for l in range(levels):
                q_left, q, q_right = sides(lambda i: tracer_ref[g, l, :, at(i)], d)
                flux = behind * q[:-1] + ahead * q[1:]
                flux_low = jnp.concatenate([none, flux], axis=0)
                flux_up = jnp.concatenate([flux, none], axis=0)
                south = south_low * q_left + south_high * q
                north = north_low * q + north_high * q_right
                out_ref[d, g, l] = q - (flux_up - flux_low) - (north - south)
        return carry

    lax.fori_loop(0, members, member, 0)


def interior(rates, tracer, east, north, bands):
    members, levels, cols, length = tracer.shape
    vmem = pl.BlockSpec(memory_space=pltpu.VMEM)
    return pl.pallas_call(
        interior_kernel,
        out_shape=jax.ShapeDtypeStruct((bands, members, levels, cols, LANES), jnp.float32),
        in_specs=[pl.BlockSpec(memory_space=pltpu.SMEM)] + [vmem] * 3,
        out_specs=vmem,
        compiler_params=pltpu.CompilerParams(vmem_limit_bytes=VMEM_BYTES),
        cost_estimate=pl.CostEstimate(
            flops=16_000_000, bytes_accessed=4_500_000, transcendentals=0
        ),
        name="interior",
    )(*in_hbm(rates), tracer, east, north)


def border_kernel(
    rate_ref, inner_ref, outer_ref, got_inner_ref, got_outer_ref, in_ref, out_ref
):
    bands, members, levels, cols, lanes = in_ref.shape
    me = lax.axis_index("member")
    first_core = (lax.axis_index("domain") & 1) == 0
    row = lax.broadcasted_iota(jnp.int32, (cols, lanes), 0)

    def member(g, carry):
        rate = rate_ref[me * members + g]

        def plane(p):
            at = pl.ds(p * bands, bands)
            inner, outer = inner_ref[g, at], outer_ref[g, at]
            got_inner, got_outer = got_inner_ref[g, at], got_outer_ref[g, at]
            return (
                jnp.where(first_core, got_outer, got_inner),
                jnp.where(first_core, outer, inner),
                jnp.where(first_core, inner, outer),
                jnp.where(first_core, got_inner, got_outer),
            )

        u_below, u_first, u_last, u_above = plane(levels)
        enter = face_weights(u_below, u_first, rate)
        leave = face_weights(u_last, u_above, rate)
        for l in range(levels):
            below, first, last, above = plane(l)
            low = enter[0] * below + enter[1] * first
            high = leave[0] * last + leave[1] * above
            for d in range(bands):
                change = jnp.where(
                    row == 0, low[d : d + 1], jnp.where(row == cols - 1, -high[d : d + 1], 0.0)
                )
                out_ref[d, g, l] = in_ref[d, g, l] + change
        return carry

    lax.fori_loop(0, members, member, 0)


def add_border(rates, inner, outer, got_inner, got_outer, blocks):
    vmem = pl.BlockSpec(memory_space=pltpu.VMEM)
    return pl.pallas_call(
        border_kernel,
        out_shape=jax.ShapeDtypeStruct(blocks.shape, jnp.float32),
        in_specs=[pl.BlockSpec(memory_space=pltpu.SMEM)] + [vmem] * 5,
        out_specs=vmem,
        compiler_params=pltpu.CompilerParams(vmem_limit_bytes=VMEM_BYTES),
        cost_estimate=pl.CostEstimate(flops=1_000_000, bytes_accessed=3_000_000, transcendentals=0),
        name="add_border",
    )(*in_hbm(rates), inner, outer, got_inner, got_outer, blocks)


def innovations(priors, values, errors):
    members = priors.shape[0]
    average = jnp.sum(priors, axis=0, keepdims=True) / members
    spread = priors - average
    variance = jnp.sum(spread * spread, axis=0, keepdims=True) / (members - 1)
    divisor = variance + errors
    reduction = 1.0 / (1.0 + jnp.sqrt(errors / divisor))
    factor = 1.0 / ((members - 1) * divisor)
    return (spread, values - average, reduction, factor)


def solve(priors, meta_ref, value_ref, error_ref, out_ref):
    members, total = priors.shape
    meta = meta_ref[...].astype(jnp.float32)
    across = jnp.concatenate(
        [meta, jnp.zeros((total - meta.shape[0], total), jnp.float32)], axis=0
    ).T
    level_j, x_j, y_j, ox_j, oy_j = (across[:, i : i + 1] for i in range(5))
    level_k, x_k, y_k = (meta[i : i + 1] for i in range(3))
    j_ids = lax.broadcasted_iota(jnp.int32, (total, total), 0)
    k_ids = lax.broadcasted_iota(jnp.int32, (total, total), 1)
    source = j_ids.astype(jnp.float32)
    taper_x = jnp.where(
        (x_k >= ox_j) & (x_k < ox_j + TILE_X), 1.0 - jnp.abs(x_k - x_j) / TILE_X, 0.0
    )
    taper_y = jnp.where(
        (y_k >= oy_j) & (y_k < oy_j + TILE_Y), 1.0 - jnp.abs(y_k - y_j) / TILE_Y, 0.0
    )
    weight = jnp.where(level_j == level_k, 1.0, 0.5) * taper_x * taper_y
    weight = jnp.where(j_ids < k_ids, weight, 0.0)
    pending = jnp.where(weight != 0.0, source, -1.0)
    values = lane_row(value_ref)
    errors = lane_row(error_ref)

    def following(done):
        return jnp.min(jnp.where(pending > done, pending, NONE), axis=0, keepdims=True)

    def step(carry):
        priors, nxt, left = carry
        spread, offset, reduction, factor = innovations(priors, values, errors)
        final = jnp.where(nxt == NONE, 1.0, 0.0)
        table = jnp.concatenate(
            [spread, offset, reduction, factor, final, jnp.zeros((12, total), jnp.float32)], axis=0
        )
        high = table.astype(jnp.bfloat16)
        rest = table - high.astype(jnp.float32)
        middle = rest.astype(jnp.bfloat16)
        low = (rest - middle.astype(jnp.float32)).astype(jnp.bfloat16)
        chosen = source == nxt
        pick = jnp.where(chosen, 1.0, 0.0).astype(jnp.bfloat16)
        dot = lambda part: jnp.dot(part, pick, preferred_element_type=jnp.float32)
        got = dot(high) + dot(middle) + dot(low)
        their_spread = got[:members]
        their_offset, their_reduction, their_factor, ready = (
            got[members + i : members + i + 1] for i in range(4)
        )
        rho = jnp.sum(jnp.where(chosen, weight, 0.0), axis=0, keepdims=True)
        covariance = jnp.sum(priors * their_spread, axis=0, keepdims=True)
        go = ready > 0.5
        scale = jnp.where(go, rho * covariance * their_factor, 0.0)
        priors = priors + scale * (their_offset - their_reduction * their_spread)
        done = jnp.where(go, nxt, nxt - 0.5)
        nxt = following(done)
        return (priors, nxt, jnp.min(nxt))

    nxt = following(jnp.full((1, total), -1.0, jnp.float32))
    priors, _, _ = lax.while_loop(
        lambda carry: carry[2] < NONE, step, (priors, nxt, jnp.min(nxt))
    )
    spread, offset, reduction, factor = innovations(priors, values, errors)
    out_ref[0] = spread * factor
    out_ref[1] = offset - reduction * spread


def apply_kernel(
    local_members, meta_ref, lanes_ref, near_ref, far_ref, value_ref, error_ref, in_ref,
    out_ref, table_ref, work, gain, sems
):
    members, levels, cols, rows = work.shape
    priors = jnp.concatenate([near_ref[...], far_ref[...]], axis=0)
    solve(priors, lanes_ref, value_ref, error_ref, table_ref)
    part = 8
    me = lax.axis_index("member")
    base = lax.axis_index("domain") * cols
    row0 = me * rows
    lane = lax.broadcasted_iota(jnp.int32, (1, LANES), 1)
    ox = lanes_ref[3:4]
    oy = lanes_ref[4:5]
    in_rows = (oy < row0 + rows) & (oy + TILE_Y > row0)
    half = members // local_members // 2

    def taper(position, centre, first, span):
        inside = (position >= first) & (position < first + span)
        return jnp.where(inside, 1.0 - jnp.abs(position - centre).astype(jnp.float32) / span, 0.0)

    def member_row(m):
        offset = (m // local_members) ^ me
        return ((offset >> 1) + half * (offset & 1)) * local_members + m % local_members

    keys = jnp.where(in_rows & (ox < base + cols) & (ox + TILE_X > base), lane, LAST)
    row_ids = row0 + lax.broadcasted_iota(jnp.int32, (part, rows), 1)
    near_ids = base + lax.broadcasted_iota(jnp.int32, (part, rows), 0)
    groups = cols // part
    band = lambda g: pl.ds(g * part, part)
    places = [(l, g) for l in range(levels) for g in range(groups)]

    def ready(k, slot):
        shift = (LANES - k) & 127
        for i in range(2):
            column = pltpu.roll(table_ref[i], shift, 1)[:, 0:1]
            gain[slot, i] = jnp.broadcast_to(column, (members, LANES))

    def update(k, slot, source):
        following = jnp.min(jnp.where(keys > k, keys, LAST))
        along = taper(row_ids, meta_ref[2, k], meta_ref[4, k], TILE_Y)
        weights = [
            taper(near_ids + g * part, meta_ref[1, k], meta_ref[3, k], TILE_X) * along
            for g in range(groups)
        ]
        sums = {}
        for m in range(members):
            s = gain[slot, 0, pl.ds(member_row(m), 1)]
            for l, g in places:
                term = source[m, l, band(g)] * s
                sums[l, g] = sums[l, g] + term if m else term
        scale = {}
        for l, g in places:
            vertical = jnp.where(meta_ref[0, k] == l, 1.0, 0.5)
            scale[l, g] = vertical * weights[g] * sums[l, g]
        ready(following, 1 - slot)
        for m in range(members):
            c = gain[slot, 1, pl.ds(member_row(m), 1)]
            for l, g in places:
                work[m, l, band(g)] = source[m, l, band(g)] + scale[l, g] * c
        return (following, 1 - slot)

    first = jnp.min(keys)
    store = lambda source: pltpu.make_async_copy(source, out_ref, sems.at[0])

    @pl.when(first < LAST)
    def _():
        ready(first, 0)
        second = update(first, 0, in_ref)
        lax.while_loop(lambda at: at[0] < LAST, lambda at: update(*at, work), second)
        store(work).start()

    @pl.when(first == LAST)
    def _():
        store(in_ref).start()

    store(work).wait()


def apply_updates(meta, near, far, values, errors, block, local_members):
    members, levels, cols, rows = block.shape
    vmem = pl.BlockSpec(memory_space=pltpu.VMEM)
    return pl.pallas_call(
        functools.partial(apply_kernel, local_members),
        out_shape=jax.ShapeDtypeStruct(block.shape, jnp.float32),
        in_specs=[pl.BlockSpec(memory_space=pltpu.SMEM)] + [vmem] * 6,
        out_specs=pl.BlockSpec(memory_space=pl.ANY),
        scratch_shapes=[
            pltpu.VMEM((2, members, LANES), jnp.float32),
            pltpu.VMEM(block.shape, jnp.float32),
            pltpu.VMEM((2, 2, members, LANES), jnp.float32),
            pltpu.SemaphoreType.DMA((1,)),
        ],
        compiler_params=pltpu.CompilerParams(vmem_limit_bytes=VMEM_BYTES),
        name="apply_updates",
    )(*in_hbm(meta), meta, near, far, *in_hbm(values, errors), block)


def exchange(array, axis, peers, reach):
    return lax.ppermute(array, axis, [(i, i ^ reach) for i in range(peers)])


def finish_priors(picked, meta, rates, cols):
    whole, q, u, q_far, u_far = (picked[:, i] for i in range(PLANES))
    place = meta[1:2] & (cols - 1)
    rate = rates[:, None]
    low = face_flux(u_far, u, q_far, q, rate)
    high = face_flux(u, u_far, q, q_far, rate)
    return whole + jnp.where(place == 0, low, 0.0) - jnp.where(place == cols - 1, high, 0.0)


def local(
    tracer, east_speed, north_speed, diffusivity, obs_cell, tile_offset, obs_value, obs_error
):
    members, levels, cols, length = tracer.shape
    bands = lax.axis_size("member")
    domains = lax.axis_size("domain")
    cells = obs_cell.transpose(2, 0, 1)
    tiles = tile_offset.transpose(0, 2, 1)
    rates = lax.dynamic_slice_in_dim(diffusivity, lax.axis_index("member") * members, members)
    inner, outer, meta, tracer, east, north = prepare(
        cells, tiles, diffusivity, tracer, east_speed, north_speed, domains
    )
    edges = inner.shape[1] - 8
    got_inner = exchange(inner, "domain", domains, 1)
    picked = inner[:, edges:] + got_inner[:, edges:]
    outer = jnp.concatenate([outer[:, :edges], picked], axis=1)

    def widen(picked, step):
        pairs = [((i + step if i % 2 else i - step) % domains, i) for i in range(domains)]
        return lax.ppermute(picked, "domain", pairs)

    pairs = [(i, (i + 1) % domains if i % 2 else (i - 1) % domains) for i in range(domains)]
    got_outer = lax.ppermute(outer, "domain", pairs)
    far = [widen(picked, step) for step in STEPS]
    tracer, east, north, _ = lax.optimization_barrier((tracer, east, north, outer))
    blocks = interior(diffusivity, tracer, east, north, bands)
    got_outer, far, blocks = lax.optimization_barrier((got_outer, far, blocks))
    picked = picked + got_outer[:, edges:] + sum(far)
    blocks = add_border(diffusivity, inner, outer, got_inner, got_outer, blocks)
    blocks, picked = lax.optimization_barrier((blocks, picked))
    block = lax.all_to_all(blocks, "member", split_axis=0, concat_axis=0, tiled=True)
    block = block.reshape(bands * members, levels, cols, length // bands)
    first = picked
    for step in range(8, domains, 8):
        picked = picked + widen(first, step)
    priors = finish_priors(picked, meta, rates, cols)
    near = jnp.concatenate(
        [priors] + [exchange(priors, "member", bands, reach) for reach in range(2, bands, 2)],
        axis=0,
    )
    far = exchange(near, "member", bands, 1)
    return apply_updates(meta, near, far, obs_value, obs_error, block, members)


def solution(mesh):
    placed = (
        P("member", None, "domain", None),
        P("member", "domain", None),
        P("member", "domain", None),
        P(),
        P(),
        P(),
        P(),
        P(),
    )
    return jax.shard_map(
        local,
        mesh=mesh,
        in_specs=placed,
        out_specs=P(None, None, "domain", "member"),
        check_vma=False,
    )
```

```python
import functools

import jax
import jax.numpy as jnp
from jax import lax
from jax.experimental import pallas as pl
from jax.experimental.pallas import tpu as pltpu
from jax.sharding import PartitionSpec as P

TILE_X = 32
TILE_Y = 64
LANES = 128
NONE = 999.0
LAST = 0x7FFFFFFF
PLANES = 5
STEPS = (4, 6)
VMEM_BYTES = 32 * 1024 * 1024


def lane_row(ref, *index):
    return jnp.concatenate([ref[(*index, slice(0, 1))], ref[(*index, slice(1, 2))]], axis=1)


def copies(pairs, sems):
    made = [pltpu.make_async_copy(src, dst, sems.at[i]) for i, (src, dst) in enumerate(pairs)]
    for one in made:
        one.start()
    return made


def face_flux(u_low, u_high, q_low, q_high, rate):
    face = 0.5 * (u_low + u_high)
    return (
        jnp.maximum(face, 0.0) * q_low + jnp.minimum(face, 0.0) * q_high - rate * (q_high - q_low)
    )


def prepare_kernel(
    domains, cell_hbm, tile_hbm, rate_hbm, tracer_hbm, east_hbm, north_hbm,
    inner_ref, outer_ref, meta_ref, tracer_ref, east_ref, north_ref,
    cell_ref, tile_ref, rate_ref, sems,
):
    members, levels, cols, length = tracer_ref.shape
    bands = length // LANES
    small = copies(
        [(cell_hbm, cell_ref), (tile_hbm, tile_ref), (rate_hbm, rate_ref)], sems.at[0]
    )
    loads = copies(
        [(tracer_hbm, tracer_ref), (east_hbm, east_ref), (north_hbm, north_ref)], sems.at[1]
    )
    for one in small:
        one.wait()
    domain = lax.axis_index("domain")
    me = lax.axis_index("member")
    col0 = domain * cols
    width = domains * cols
    level = lane_row(cell_ref, 0)
    x = lane_row(cell_ref, 1)
    y = lane_row(cell_ref, 2)
    ox = jnp.concatenate([tile_ref[0, 0:1], tile_ref[1, 0:1]], axis=1)
    oy = jnp.concatenate([tile_ref[0, 1:2], tile_ref[1, 1:2]], axis=1)
    lane = lax.broadcasted_iota(jnp.int32, (1, LANES), 1)
    zero = jnp.zeros((3, LANES), jnp.int32)
    meta_ref[...] = jnp.concatenate([level, x, y, ox, oy, zero], axis=0)
    near = (x >= col0) & (x < col0 + cols)
    before = jnp.where(col0 == 0, width, col0) - 1
    after = jnp.where(col0 + cols == width, 0, col0 + cols)
    near = near | (x == before) | (x == after)
    keys = jnp.where(near, (lane << 21) + (level << 19) + (x << 10) + y, LAST)
    for one in loads:
        one.wait()
    first_core = (domain & 1) == 0
    for p in range(levels + 1):
        for d in range(bands):
            at = slice(d * LANES, (d + 1) * LANES)
            plane = tracer_ref.at[:, p] if p < levels else east_ref
            low = plane[:, 0, at]
            high = plane[:, cols - 1, at]
            inner_ref[:, p * bands + d] = jnp.where(first_core, high, low)
            outer_ref[:, p * bands + d] = jnp.where(first_core, low, high)

    sub = lax.broadcasted_iota(jnp.int32, (members, LANES), 0)
    lanes = lax.broadcasted_iota(jnp.int32, (members, LANES), 1)
    rates = jnp.zeros((members, LANES), jnp.float32)
    for m in range(members):
        rates = jnp.where(sub == m, rate_ref[me * members + m], rates)

    def pick(carry):
        key, planes = carry
        following = jnp.min(jnp.where(keys > key, keys, LAST))
        k = key >> 21
        l = (key >> 19) & 3
        col = (key >> 10) & 511
        row = key & 1023
        own = (col >= col0) & (col < col0 + cols)
        here = jnp.where(own, col - col0, jnp.where(col == before, 0, cols - 1))

        def fetch(ref, lead, i, j):
            i = jnp.clip(i, 0, cols - 1)
            j = jnp.clip(j, 0, length - 1)
            first = pl.multiple_of((i >> 3) << 3, 8)
            start = pl.multiple_of((j >> 7) << 7, LANES)
            rows = jnp.zeros((members, LANES), jnp.float32)
            for m in range(members):
                tile = ref[(m, *lead, pl.ds(first, 8), pl.ds(start, LANES))]
                rows = jnp.where(sub == m, pltpu.roll(tile, (m - i) & 7, 0), rows)
            return pltpu.roll(rows, (k - (j & 127) + LANES) & 127, 1)

        q = fetch(tracer_ref, (l,), here, row)
        u = fetch(east_ref, (), here, row)
        v = fetch(north_ref, (), here, row)
        south = face_flux(
            fetch(north_ref, (), here, row - 1), v, fetch(tracer_ref, (l,), here, row - 1), q, rates
        )
        north = face_flux(
            v, fetch(north_ref, (), here, row + 1), q, fetch(tracer_ref, (l,), here, row + 1), rates
        )
        low = face_flux(
            fetch(east_ref, (), here - 1, row), u, fetch(tracer_ref, (l,), here - 1, row), q, rates
        )
        high = face_flux(
            u, fetch(east_ref, (), here + 1, row), q, fetch(tracer_ref, (l,), here + 1, row), rates
        )
        south = jnp.where(row == 0, 0.0, south)
        north = jnp.where(row == length - 1, 0.0, north)
        low = jnp.where(here == 0, 0.0, low)
        high = jnp.where(here == cols - 1, 0.0, high)
        mine = lanes == k
        ours = mine & own
        theirs = mine & jnp.logical_not(own)
        values = (
            (ours, q - (high - low) - (north - south)), (ours, q), (ours, u), (theirs, q), (theirs, u)
        )
        planes = tuple(jnp.where(at, new, old) for (at, new), old in zip(values, planes))
        return (following, planes)

    blank = jnp.zeros((members, LANES), jnp.float32)
    _, planes = lax.while_loop(
        lambda carry: carry[0] < LAST, pick, (jnp.min(keys), (blank,) * PLANES)
    )
    for i, plane in enumerate(planes):
        inner_ref[:, (levels + 1) * bands + i] = plane
    for i in range(PLANES, 8):
        inner_ref[:, (levels + 1) * bands + i] = blank


def in_hbm(*arrays):
    return [pltpu.with_memory_space_constraint(a, pltpu.HBM) for a in arrays]


def prepare(cells, tiles, rates, tracer, east, north, domains):
    members, levels, cols, length = tracer.shape
    vmem = pl.BlockSpec(memory_space=pltpu.VMEM)
    hbm = pl.BlockSpec(memory_space=pltpu.HBM)
    sent = jax.ShapeDtypeStruct(
        (members, (levels + 1) * (length // LANES) + 8, LANES), jnp.float32
    )
    return pl.pallas_call(
        functools.partial(prepare_kernel, domains),
        out_shape=[
            sent,
            sent,
            jax.ShapeDtypeStruct((8, LANES), jnp.int32),
            jax.ShapeDtypeStruct(tracer.shape, jnp.float32),
            jax.ShapeDtypeStruct(east.shape, jnp.float32),
            jax.ShapeDtypeStruct(north.shape, jnp.float32),
        ],
        in_specs=[hbm] * 6,
        out_specs=[vmem] * 6,
        scratch_shapes=[
            pltpu.VMEM(cells.shape, jnp.int32),
            pltpu.VMEM(tiles.shape, jnp.int32),
            pltpu.SMEM(rates.shape, jnp.float32),
            pltpu.SemaphoreType.DMA((2, 3)),
        ],
        compiler_params=pltpu.CompilerParams(vmem_limit_bytes=VMEM_BYTES),
        cost_estimate=pl.CostEstimate(flops=1_000_000, bytes_accessed=3_000_000, transcendentals=0),
        name="prepare",
    )(*in_hbm(cells, tiles, rates, tracer, east, north))


def face_weights(low, high, rate):
    face = 0.5 * (low + high)
    return (jnp.maximum(face, 0.0) + rate, jnp.minimum(face, 0.0) - rate)


def interior_kernel(rate_ref, tracer_ref, east_ref, north_ref, out_ref):
    members, levels, cols, length = tracer_ref.shape
    bands = out_ref.shape[0]
    me = lax.axis_index("member")
    lane = lax.broadcasted_iota(jnp.int32, (cols, LANES), 1)
    none = jnp.zeros((1, LANES), jnp.float32)

    def sides(read, d):
        here = read(d)
        left = jnp.where(lane == LANES - 1, read(d - 1), here) if d else here
        right = jnp.where(lane == 0, read(d + 1), here) if d < bands - 1 else here
        return (pltpu.roll(left, 1, 1), here, pltpu.roll(right, LANES - 1, 1))

    def member(g, carry):
        rate = rate_ref[me * members + g]
        for d in range(bands):
            at = lambda i: pl.ds(i * LANES, LANES)
            u = east_ref[g, :, at(d)]
            behind, ahead = face_weights(u[:-1], u[1:], rate)
            v_left, v, v_right = sides(lambda i: north_ref[g, :, at(i)], d)
            south_low, south_high = face_weights(v_left, v, rate)
            north_low, north_high = face_weights(v, v_right, rate)
            if d == 0:
                south_low = jnp.where(lane == 0, 0.0, south_low)
                south_high = jnp.where(lane == 0, 0.0, south_high)
            if d == bands - 1:
                north_low = jnp.where(lane == LANES - 1, 0.0, north_low)
                north_high = jnp.where(lane == LANES - 1, 0.0, north_high)
            for l in range(levels):
                q_left, q, q_right = sides(lambda i: tracer_ref[g, l, :, at(i)], d)
                flux = behind * q[:-1] + ahead * q[1:]
                flux_low = jnp.concatenate([none, flux], axis=0)
                flux_up = jnp.concatenate([flux, none], axis=0)
                south = south_low * q_left + south_high * q
                north = north_low * q + north_high * q_right
                out_ref[d, g, l] = q - (flux_up - flux_low) - (north - south)
        return carry

    lax.fori_loop(0, members, member, 0)


def interior(rates, tracer, east, north, bands):
    members, levels, cols, length = tracer.shape
    vmem = pl.BlockSpec(memory_space=pltpu.VMEM)
    return pl.pallas_call(
        interior_kernel,
        out_shape=jax.ShapeDtypeStruct((bands, members, levels, cols, LANES), jnp.float32),
        in_specs=[pl.BlockSpec(memory_space=pltpu.SMEM)] + [vmem] * 3,
        out_specs=vmem,
        compiler_params=pltpu.CompilerParams(vmem_limit_bytes=VMEM_BYTES),
        cost_estimate=pl.CostEstimate(
            flops=16_000_000, bytes_accessed=4_500_000, transcendentals=0
        ),
        name="interior",
    )(*in_hbm(rates), tracer, east, north)


def border_kernel(
    rate_ref, inner_ref, outer_ref, got_inner_ref, got_outer_ref, in_ref, out_ref
):
    bands, members, levels, cols, lanes = in_ref.shape
    me = lax.axis_index("member")
    first_core = (lax.axis_index("domain") & 1) == 0
    row = lax.broadcasted_iota(jnp.int32, (8, lanes), 0)

    def member(g, carry):
        rate = rate_ref[me * members + g]

        def plane(p):
            at = pl.ds(p * bands, bands)
            inner, outer = inner_ref[g, at], outer_ref[g, at]
            got_inner, got_outer = got_inner_ref[g, at], got_outer_ref[g, at]
            return (
                jnp.where(first_core, got_outer, got_inner),
                jnp.where(first_core, outer, inner),
                jnp.where(first_core, inner, outer),
                jnp.where(first_core, got_inner, got_outer),
            )

        u_below, u_first, u_last, u_above = plane(levels)
        enter = face_weights(u_below, u_first, rate)
        leave = face_weights(u_last, u_above, rate)
        for l in range(levels):
            below, first, last, above = plane(l)
            low = enter[0] * below + enter[1] * first
            high = leave[0] * last + leave[1] * above
            for d in range(bands):
                at = slice(d, d + 1)
                top = jnp.where(row == 0, low[at], 0.0)
                bottom = jnp.where(row == 7, high[at], 0.0)
                out_ref[d, g, l, :8] = in_ref[d, g, l, :8] + top
                if cols > 16:
                    out_ref[d, g, l, 8 : cols - 8] = in_ref[d, g, l, 8 : cols - 8]
                out_ref[d, g, l, cols - 8 :] = in_ref[d, g, l, cols - 8 :] - bottom
        return carry

    lax.fori_loop(0, members, member, 0, unroll=4)


def add_border(rates, inner, outer, got_inner, got_outer, blocks):
    vmem = pl.BlockSpec(memory_space=pltpu.VMEM)
    return pl.pallas_call(
        border_kernel,
        out_shape=jax.ShapeDtypeStruct(blocks.shape, jnp.float32),
        in_specs=[pl.BlockSpec(memory_space=pltpu.SMEM)] + [vmem] * 5,
        out_specs=vmem,
        compiler_params=pltpu.CompilerParams(vmem_limit_bytes=VMEM_BYTES),
        cost_estimate=pl.CostEstimate(flops=1_000_000, bytes_accessed=3_000_000, transcendentals=0),
        name="add_border",
    )(*in_hbm(rates), inner, outer, got_inner, got_outer, blocks)


def innovations(priors, values, errors):
    members = priors.shape[0]
    average = jnp.sum(priors, axis=0, keepdims=True) / members
    spread = priors - average
    variance = jnp.sum(spread * spread, axis=0, keepdims=True) / (members - 1)
    divisor = variance + errors
    reduction = 1.0 / (1.0 + jnp.sqrt(errors / divisor))
    factor = 1.0 / ((members - 1) * divisor)
    return (spread, values - average, reduction, factor)


def solve(priors, meta_ref, value_ref, error_ref, out_ref):
    members, total = priors.shape
    meta = meta_ref[...].astype(jnp.float32)
    across = jnp.concatenate(
        [meta, jnp.zeros((total - meta.shape[0], total), jnp.float32)], axis=0
    ).T
    level_j, x_j, y_j, ox_j, oy_j = (across[:, i : i + 1] for i in range(5))
    level_k, x_k, y_k = (meta[i : i + 1] for i in range(3))
    j_ids = lax.broadcasted_iota(jnp.int32, (total, total), 0)
    k_ids = lax.broadcasted_iota(jnp.int32, (total, total), 1)
    source = j_ids.astype(jnp.float32)
    taper_x = jnp.where(
        (x_k >= ox_j) & (x_k < ox_j + TILE_X), 1.0 - jnp.abs(x_k - x_j) / TILE_X, 0.0
    )
    taper_y = jnp.where(
        (y_k >= oy_j) & (y_k < oy_j + TILE_Y), 1.0 - jnp.abs(y_k - y_j) / TILE_Y, 0.0
    )
    weight = jnp.where(level_j == level_k, 1.0, 0.5) * taper_x * taper_y
    weight = jnp.where(j_ids < k_ids, weight, 0.0)
    pending = jnp.where(weight != 0.0, source, -1.0)
    values = lane_row(value_ref)
    errors = lane_row(error_ref)

    def following(done):
        return jnp.min(jnp.where(pending > done, pending, NONE), axis=0, keepdims=True)

    def step(carry):
        priors, nxt, left = carry
        spread, offset, reduction, factor = innovations(priors, values, errors)
        final = jnp.where(nxt == NONE, 1.0, 0.0)
        table = jnp.concatenate(
            [spread, offset, reduction, factor, final, jnp.zeros((12, total), jnp.float32)], axis=0
        )
        high = table.astype(jnp.bfloat16)
        rest = table - high.astype(jnp.float32)
        middle = rest.astype(jnp.bfloat16)
        low = (rest - middle.astype(jnp.float32)).astype(jnp.bfloat16)
        chosen = source == nxt
        pick = jnp.where(chosen, 1.0, 0.0).astype(jnp.bfloat16)
        dot = lambda part: jnp.dot(part, pick, preferred_element_type=jnp.float32)
        got = dot(high) + dot(middle) + dot(low)
        their_spread = got[:members]
        their_offset, their_reduction, their_factor, ready = (
            got[members + i : members + i + 1] for i in range(4)
        )
        rho = jnp.sum(jnp.where(chosen, weight, 0.0), axis=0, keepdims=True)
        covariance = jnp.sum(priors * their_spread, axis=0, keepdims=True)
        go = ready > 0.5
        scale = jnp.where(go, rho * covariance * their_factor, 0.0)
        priors = priors + scale * (their_offset - their_reduction * their_spread)
        done = jnp.where(go, nxt, nxt - 0.5)
        nxt = following(done)
        return (priors, nxt, jnp.min(nxt))

    nxt = following(jnp.full((1, total), -1.0, jnp.float32))
    priors, _, _ = lax.while_loop(
        lambda carry: carry[2] < NONE, step, (priors, nxt, jnp.min(nxt))
    )
    spread, offset, reduction, factor = innovations(priors, values, errors)
    out_ref[0] = spread * factor
    out_ref[1] = offset - reduction * spread


def apply_kernel(
    local_members, meta_ref, lanes_ref, value_ref, error_ref, in_ref, *refs
):
    *parts, out_ref, table_ref, work, gain, sems = refs
    members, levels, cols, rows = work.shape
    priors = jnp.concatenate([one[...] for one in parts], axis=0)
    solve(priors, lanes_ref, value_ref, error_ref, table_ref)
    part = 8
    me = lax.axis_index("member")
    base = lax.axis_index("domain") * cols
    row0 = me * rows
    lane = lax.broadcasted_iota(jnp.int32, (1, LANES), 1)
    ox = lanes_ref[3:4]
    oy = lanes_ref[4:5]
    in_rows = (oy < row0 + rows) & (oy + TILE_Y > row0)

    def taper(position, centre, first, span):
        inside = (position >= first) & (position < first + span)
        return jnp.where(inside, 1.0 - jnp.abs(position - centre).astype(jnp.float32) / span, 0.0)

    def member_row(m):
        return ((m // local_members) ^ me) * local_members + m % local_members

    keys = jnp.where(in_rows & (ox < base + cols) & (ox + TILE_X > base), lane, LAST)
    row_ids = row0 + lax.broadcasted_iota(jnp.int32, (part, rows), 1)
    near_ids = base + lax.broadcasted_iota(jnp.int32, (part, rows), 0)
    groups = cols // part
    band = lambda g: pl.ds(g * part, part)
    places = [(l, g) for l in range(levels) for g in range(groups)]

    def ready(k, slot):
        shift = (LANES - k) & 127
        for i in range(2):
            column = pltpu.roll(table_ref[i], shift, 1)[:, 0:1]
            gain[slot, i] = jnp.broadcast_to(column, (members, LANES))

    def update(k, slot, source):
        following = jnp.min(jnp.where(keys > k, keys, LAST))
        along = taper(row_ids, meta_ref[2, k], meta_ref[4, k], TILE_Y)
        weights = [
            taper(near_ids + g * part, meta_ref[1, k], meta_ref[3, k], TILE_X) * along
            for g in range(groups)
        ]
        sums = {}
        for m in range(members):
            s = gain[slot, 0, pl.ds(member_row(m), 1)]
            for l, g in places:
                term = source[m, l, band(g)] * s
                sums[l, g] = sums[l, g] + term if m else term
        scale = {}
        for l, g in places:
            vertical = jnp.where(meta_ref[0, k] == l, 1.0, 0.5)
            scale[l, g] = vertical * weights[g] * sums[l, g]
        ready(following, 1 - slot)
        for m in range(members):
            c = gain[slot, 1, pl.ds(member_row(m), 1)]
            for l, g in places:
                work[m, l, band(g)] = source[m, l, band(g)] + scale[l, g] * c
        return (following, 1 - slot)

    first = jnp.min(keys)
    store = lambda source: pltpu.make_async_copy(source, out_ref, sems.at[0])

    @pl.when(first < LAST)
    def _():
        ready(first, 0)
        second = update(first, 0, in_ref)
        lax.while_loop(lambda at: at[0] < LAST, lambda at: update(*at, work), second)
        store(work).start()

    @pl.when(first == LAST)
    def _():
        store(in_ref).start()

    store(work).wait()


def apply_updates(meta, parts, values, errors, block, local_members):
    members, levels, cols, rows = block.shape
    vmem = pl.BlockSpec(memory_space=pltpu.VMEM)
    return pl.pallas_call(
        functools.partial(apply_kernel, local_members),
        out_shape=jax.ShapeDtypeStruct(block.shape, jnp.float32),
        in_specs=[pl.BlockSpec(memory_space=pltpu.SMEM)] + [vmem] * (4 + len(parts)),
        out_specs=pl.BlockSpec(memory_space=pl.ANY),
        scratch_shapes=[
            pltpu.VMEM((2, members, LANES), jnp.float32),
            pltpu.VMEM(block.shape, jnp.float32),
            pltpu.VMEM((2, 2, members, LANES), jnp.float32),
            pltpu.SemaphoreType.DMA((1,)),
        ],
        compiler_params=pltpu.CompilerParams(vmem_limit_bytes=VMEM_BYTES),
        name="apply_updates",
    )(*in_hbm(meta), meta, *in_hbm(values, errors), block, *parts)


def exchange(array, axis, peers, reach):
    return lax.ppermute(array, axis, [(i, i ^ reach) for i in range(peers)])


def finish_priors(picked, meta, rates, cols):
    whole, q, u, q_far, u_far = (picked[i] for i in range(PLANES))
    place = meta[1:2] & (cols - 1)
    rate = rates[:, None]
    low = face_flux(u_far, u, q_far, q, rate)
    high = face_flux(u, u_far, q, q_far, rate)
    return whole + jnp.where(place == 0, low, 0.0) - jnp.where(place == cols - 1, high, 0.0)


def local(
    tracer, east_speed, north_speed, diffusivity, obs_cell, tile_offset, obs_value, obs_error
):
    members, levels, cols, length = tracer.shape
    bands = lax.axis_size("member")
    domains = lax.axis_size("domain")
    cells = obs_cell.transpose(2, 0, 1)
    tiles = tile_offset.transpose(0, 2, 1)
    me = lax.axis_index("member")
    rates = jnp.concatenate(
        [lax.dynamic_slice_in_dim(diffusivity, at * members, members) for at in (me, me ^ 1)]
    )
    inner, outer, meta, tracer, east, north = prepare(
        cells, tiles, diffusivity, tracer, east_speed, north_speed, domains
    )
    edges = inner.shape[1] - 8
    got_inner = exchange(inner, "domain", domains, 1)
    picked = inner[:, edges:] + got_inner[:, edges:]
    outer = jnp.concatenate([outer[:, :edges], picked], axis=1)

    def widen(picked, step):
        pairs = [((i + step if i % 2 else i - step) % domains, i) for i in range(domains)]
        return lax.ppermute(picked, "domain", pairs)

    pairs = [(i, (i + 1) % domains if i % 2 else (i - 1) % domains) for i in range(domains)]
    got_outer = lax.ppermute(outer, "domain", pairs)
    far = [widen(picked, step) for step in STEPS]
    tracer, east, north, _ = lax.optimization_barrier((tracer, east, north, outer))
    blocks = interior(diffusivity, tracer, east, north, bands)
    got_outer, far, blocks = lax.optimization_barrier((got_outer, far, blocks))
    picked = (picked + got_outer[:, edges:] + sum(far)).transpose(1, 0, 2)[:PLANES]
    picked = jnp.concatenate([picked, exchange(picked, "member", bands, 1)], axis=1)
    blocks = add_border(diffusivity, inner, outer, got_inner, got_outer, blocks)
    blocks, picked = lax.optimization_barrier((blocks, picked))
    block = lax.all_to_all(blocks, "member", split_axis=0, concat_axis=0, tiled=True)
    block = block.reshape(bands * members, levels, cols, length // bands)
    first = picked
    for step in range(8, domains, 8):
        picked = picked + widen(first, step)
    priors = finish_priors(picked, meta, rates, cols)
    parts = [priors] + [exchange(priors, "member", bands, reach) for reach in range(2, bands, 2)]
    return apply_updates(meta, parts, obs_value, obs_error, block, members)


def solution(mesh):
    placed = (
        P("member", None, "domain", None),
        P("member", "domain", None),
        P("member", "domain", None),
        P(),
        P(),
        P(),
        P(),
        P(),
    )
    return jax.shard_map(
        local,
        mesh=mesh,
        in_specs=placed,
        out_specs=P(None, None, "domain", "member"),
        check_vma=False,
    )
```

```python
import functools

import jax
import jax.numpy as jnp
from jax import lax
from jax.experimental import pallas as pl
from jax.experimental.pallas import tpu as pltpu
from jax.sharding import PartitionSpec as P

TILE_X = 32
TILE_Y = 64
LANES = 128
NONE = 999.0
LAST = 0x7FFFFFFF
PLANES = 5
CHUNKS = 4
STEPS = (4, -2)
VMEM_BYTES = 32 * 1024 * 1024


def lane_row(ref, *index):
    return jnp.concatenate([ref[(*index, slice(0, 1))], ref[(*index, slice(1, 2))]], axis=1)


def copies(pairs, sems):
    made = [pltpu.make_async_copy(src, dst, sems.at[i]) for i, (src, dst) in enumerate(pairs)]
    for one in made:
        one.start()
    return made


def face_flux(u_low, u_high, q_low, q_high, rate):
    face = 0.5 * (u_low + u_high)
    return (
        jnp.maximum(face, 0.0) * q_low + jnp.minimum(face, 0.0) * q_high - rate * (q_high - q_low)
    )


def prepare_kernel(
    domains, cell_hbm, tile_hbm, rate_hbm, tracer_hbm, east_hbm, north_hbm,
    inner_ref, outer_ref, meta_ref, tracer_ref, east_ref, north_ref,
    cell_ref, tile_ref, rate_ref, sems,
):
    members, levels, cols, length = tracer_ref.shape
    bands = length // LANES
    small = copies(
        [(cell_hbm, cell_ref), (tile_hbm, tile_ref), (rate_hbm, rate_ref)], sems.at[0]
    )
    loads = copies(
        [(tracer_hbm, tracer_ref), (east_hbm, east_ref), (north_hbm, north_ref)], sems.at[1]
    )
    for one in small:
        one.wait()
    domain = lax.axis_index("domain")
    me = lax.axis_index("member")
    col0 = domain * cols
    width = domains * cols
    level = lane_row(cell_ref, 0)
    x = lane_row(cell_ref, 1)
    y = lane_row(cell_ref, 2)
    ox = jnp.concatenate([tile_ref[0, 0:1], tile_ref[1, 0:1]], axis=1)
    oy = jnp.concatenate([tile_ref[0, 1:2], tile_ref[1, 1:2]], axis=1)
    lane = lax.broadcasted_iota(jnp.int32, (1, LANES), 1)
    zero = jnp.zeros((3, LANES), jnp.int32)
    meta_ref[...] = jnp.concatenate([level, x, y, ox, oy, zero], axis=0)
    near = (x >= col0) & (x < col0 + cols)
    before = jnp.where(col0 == 0, width, col0) - 1
    after = jnp.where(col0 + cols == width, 0, col0 + cols)
    near = near | (x == before) | (x == after)
    keys = jnp.where(near, (lane << 21) + (level << 19) + (x << 10) + y, LAST)
    for one in loads:
        one.wait()
    first_core = (domain & 1) == 0
    for p in range(levels + 1):
        for d in range(bands):
            at = slice(d * LANES, (d + 1) * LANES)
            plane = tracer_ref.at[:, p] if p < levels else east_ref
            low = plane[:, 0, at]
            high = plane[:, cols - 1, at]
            inner_ref[:, p * bands + d] = jnp.where(first_core, high, low)
            outer_ref[:, p * bands + d] = jnp.where(first_core, low, high)

    sub = lax.broadcasted_iota(jnp.int32, (members, LANES), 0)
    lanes = lax.broadcasted_iota(jnp.int32, (members, LANES), 1)
    rates = jnp.zeros((members, LANES), jnp.float32)
    for m in range(members):
        rates = jnp.where(sub == m, rate_ref[me * members + m], rates)

    def pick(carry):
        key, planes = carry
        following = jnp.min(jnp.where(keys > key, keys, LAST))
        k = key >> 21
        l = (key >> 19) & 3
        col = (key >> 10) & 511
        row = key & 1023
        own = (col >= col0) & (col < col0 + cols)
        here = jnp.where(own, col - col0, jnp.where(col == before, 0, cols - 1))

        def fetch(ref, lead, i, j):
            i = jnp.clip(i, 0, cols - 1)
            j = jnp.clip(j, 0, length - 1)
            first = pl.multiple_of((i >> 3) << 3, 8)
            start = pl.multiple_of((j >> 7) << 7, LANES)
            rows = jnp.zeros((members, LANES), jnp.float32)
            for m in range(members):
                tile = ref[(m, *lead, pl.ds(first, 8), pl.ds(start, LANES))]
                rows = jnp.where(sub == m, pltpu.roll(tile, (m - i) & 7, 0), rows)
            return pltpu.roll(rows, (k - (j & 127) + LANES) & 127, 1)

        q = fetch(tracer_ref, (l,), here, row)
        u = fetch(east_ref, (), here, row)
        v = fetch(north_ref, (), here, row)
        south = face_flux(
            fetch(north_ref, (), here, row - 1), v, fetch(tracer_ref, (l,), here, row - 1), q, rates
        )
        north = face_flux(
            v, fetch(north_ref, (), here, row + 1), q, fetch(tracer_ref, (l,), here, row + 1), rates
        )
        low = face_flux(
            fetch(east_ref, (), here - 1, row), u, fetch(tracer_ref, (l,), here - 1, row), q, rates
        )
        high = face_flux(
            u, fetch(east_ref, (), here + 1, row), q, fetch(tracer_ref, (l,), here + 1, row), rates
        )
        south = jnp.where(row == 0, 0.0, south)
        north = jnp.where(row == length - 1, 0.0, north)
        low = jnp.where(here == 0, 0.0, low)
        high = jnp.where(here == cols - 1, 0.0, high)
        mine = lanes == k
        ours = mine & own
        theirs = mine & jnp.logical_not(own)
        values = (
            (ours, q - (high - low) - (north - south)), (ours, q), (ours, u), (theirs, q), (theirs, u)
        )
        planes = tuple(jnp.where(at, new, old) for (at, new), old in zip(values, planes))
        return (following, planes)

    blank = jnp.zeros((members, LANES), jnp.float32)
    _, planes = lax.while_loop(
        lambda carry: carry[0] < LAST, pick, (jnp.min(keys), (blank,) * PLANES)
    )
    for i, plane in enumerate(planes):
        inner_ref[:, (levels + 1) * bands + i] = plane
    for i in range(PLANES, 8):
        inner_ref[:, (levels + 1) * bands + i] = blank


def in_hbm(*arrays):
    return [pltpu.with_memory_space_constraint(a, pltpu.HBM) for a in arrays]


def prepare(cells, tiles, rates, tracer, east, north, domains):
    members, levels, cols, length = tracer.shape
    vmem = pl.BlockSpec(memory_space=pltpu.VMEM)
    hbm = pl.BlockSpec(memory_space=pltpu.HBM)
    sent = jax.ShapeDtypeStruct(
        (members, (levels + 1) * (length // LANES) + 8, LANES), jnp.float32
    )
    return pl.pallas_call(
        functools.partial(prepare_kernel, domains),
        out_shape=[
            sent,
            sent,
            jax.ShapeDtypeStruct((8, LANES), jnp.int32),
            jax.ShapeDtypeStruct(tracer.shape, jnp.float32),
            jax.ShapeDtypeStruct(east.shape, jnp.float32),
            jax.ShapeDtypeStruct(north.shape, jnp.float32),
        ],
        in_specs=[hbm] * 6,
        out_specs=[vmem] * 6,
        scratch_shapes=[
            pltpu.VMEM(cells.shape, jnp.int32),
            pltpu.VMEM(tiles.shape, jnp.int32),
            pltpu.SMEM(rates.shape, jnp.float32),
            pltpu.SemaphoreType.DMA((2, 3)),
        ],
        compiler_params=pltpu.CompilerParams(vmem_limit_bytes=VMEM_BYTES),
        cost_estimate=pl.CostEstimate(flops=1_000_000, bytes_accessed=3_000_000, transcendentals=0),
        name="prepare",
    )(*in_hbm(cells, tiles, rates, tracer, east, north))


def face_weights(low, high, rate):
    face = 0.5 * (low + high)
    return (jnp.maximum(face, 0.0) + rate, jnp.minimum(face, 0.0) - rate)


def interior_kernel(rate_ref, tracer_ref, east_ref, north_ref, out_ref):
    members, levels, cols, length = tracer_ref.shape
    bands = out_ref.shape[0]
    me = lax.axis_index("member")
    lane = lax.broadcasted_iota(jnp.int32, (cols, LANES), 1)
    none = jnp.zeros((1, LANES), jnp.float32)

    def sides(read, d):
        here = read(d)
        left = jnp.where(lane == LANES - 1, read(d - 1), here) if d else here
        right = jnp.where(lane == 0, read(d + 1), here) if d < bands - 1 else here
        return (pltpu.roll(left, 1, 1), here, pltpu.roll(right, LANES - 1, 1))

    def member(g, carry):
        rate = rate_ref[me * members + g]
        for d in range(bands):
            at = lambda i: pl.ds(i * LANES, LANES)
            u = east_ref[g, :, at(d)]
            behind, ahead = face_weights(u[:-1], u[1:], rate)
            v_left, v, v_right = sides(lambda i: north_ref[g, :, at(i)], d)
            south_low, south_high = face_weights(v_left, v, rate)
            north_low, north_high = face_weights(v, v_right, rate)
            if d == 0:
                south_low = jnp.where(lane == 0, 0.0, south_low)
                south_high = jnp.where(lane == 0, 0.0, south_high)
            if d == bands - 1:
                north_low = jnp.where(lane == LANES - 1, 0.0, north_low)
                north_high = jnp.where(lane == LANES - 1, 0.0, north_high)
            for l in range(levels):
                q_left, q, q_right = sides(lambda i: tracer_ref[g, l, :, at(i)], d)
                flux = behind * q[:-1] + ahead * q[1:]
                flux_low = jnp.concatenate([none, flux], axis=0)
                flux_up = jnp.concatenate([flux, none], axis=0)
                south = south_low * q_left + south_high * q
                north = north_low * q + north_high * q_right
                out_ref[d, g, l] = q - (flux_up - flux_low) - (north - south)
        return carry

    lax.fori_loop(0, members, member, 0)


def interior(rates, tracer, east, north, bands):
    members, levels, cols, length = tracer.shape
    vmem = pl.BlockSpec(memory_space=pltpu.VMEM)
    return pl.pallas_call(
        interior_kernel,
        out_shape=jax.ShapeDtypeStruct((bands, members, levels, cols, LANES), jnp.float32),
        in_specs=[pl.BlockSpec(memory_space=pltpu.SMEM)] + [vmem] * 3,
        out_specs=vmem,
        compiler_params=pltpu.CompilerParams(vmem_limit_bytes=VMEM_BYTES),
        cost_estimate=pl.CostEstimate(
            flops=16_000_000, bytes_accessed=4_500_000, transcendentals=0
        ),
        name="interior",
    )(*in_hbm(rates), tracer, east, north)


def border_kernel(
    rate_ref, inner_ref, outer_ref, got_inner_ref, got_outer_ref, in_ref, out_any, out_ref, sems
):
    bands, members, levels, cols, lanes = in_ref.shape
    store = lambda g: pltpu.make_async_copy(out_ref.at[:, g], out_any.at[:, g], sems.at[g])
    me = lax.axis_index("member")
    first_core = (lax.axis_index("domain") & 1) == 0
    row = lax.broadcasted_iota(jnp.int32, (8, lanes), 0)

    def member(g, carry):
        rate = rate_ref[me * members + g]

        def plane(p):
            at = pl.ds(p * bands, bands)
            inner, outer = inner_ref[g, at], outer_ref[g, at]
            got_inner, got_outer = got_inner_ref[g, at], got_outer_ref[g, at]
            return (
                jnp.where(first_core, got_outer, got_inner),
                jnp.where(first_core, outer, inner),
                jnp.where(first_core, inner, outer),
                jnp.where(first_core, got_inner, got_outer),
            )

        u_below, u_first, u_last, u_above = plane(levels)
        enter = face_weights(u_below, u_first, rate)
        leave = face_weights(u_last, u_above, rate)
        for l in range(levels):
            below, first, last, above = plane(l)
            low = enter[0] * below + enter[1] * first
            high = leave[0] * last + leave[1] * above
            for d in range(bands):
                top = jnp.where(row == 0, pltpu.roll(low, (8 - d) % 8, 0), 0.0)
                bottom = jnp.where(row == 7, pltpu.roll(high, 7 - d, 0), 0.0)
                out_ref[d, g, l, :8] = in_ref[d, g, l, :8] + top
                if cols > 16:
                    out_ref[d, g, l, 8 : cols - 8] = in_ref[d, g, l, 8 : cols - 8]
                out_ref[d, g, l, cols - 8 :] = in_ref[d, g, l, cols - 8 :] - bottom
        store(g).start()
        return carry

    lax.fori_loop(0, members, member, 0, unroll=4)
    for g in range(members):
        store(g).wait()


def add_border(rates, inner, outer, got_inner, got_outer, blocks):
    vmem = pl.BlockSpec(memory_space=pltpu.VMEM)
    return pl.pallas_call(
        border_kernel,
        out_shape=jax.ShapeDtypeStruct(blocks.shape, jnp.float32),
        in_specs=[pl.BlockSpec(memory_space=pltpu.SMEM)] + [vmem] * 5,
        out_specs=pl.BlockSpec(memory_space=pl.ANY),
        scratch_shapes=[
            pltpu.VMEM(blocks.shape, jnp.float32),
            pltpu.SemaphoreType.DMA((blocks.shape[1],)),
        ],
        compiler_params=pltpu.CompilerParams(vmem_limit_bytes=VMEM_BYTES),
        cost_estimate=pl.CostEstimate(flops=1_000_000, bytes_accessed=3_000_000, transcendentals=0),
        name="add_border",
    )(*in_hbm(rates), inner, outer, got_inner, got_outer, blocks)


def innovations(priors, values, errors):
    members = priors.shape[0]
    average = jnp.sum(priors, axis=0, keepdims=True) / members
    spread = priors - average
    variance = jnp.sum(spread * spread, axis=0, keepdims=True) / (members - 1)
    divisor = variance + errors
    reduction = 1.0 / (1.0 + jnp.sqrt(errors / divisor))
    factor = 1.0 / ((members - 1) * divisor)
    return (spread, values - average, reduction, factor)


def solve(priors, meta_ref, value_ref, error_ref):
    members, total = priors.shape
    meta = meta_ref[...].astype(jnp.float32)
    across = jnp.concatenate(
        [meta, jnp.zeros((total - meta.shape[0], total), jnp.float32)], axis=0
    ).T
    level_j, x_j, y_j, ox_j, oy_j = (across[:, i : i + 1] for i in range(5))
    level_k, x_k, y_k = (meta[i : i + 1] for i in range(3))
    j_ids = lax.broadcasted_iota(jnp.int32, (total, total), 0)
    k_ids = lax.broadcasted_iota(jnp.int32, (total, total), 1)
    source = j_ids.astype(jnp.float32)
    taper_x = jnp.where(
        (x_k >= ox_j) & (x_k < ox_j + TILE_X), 1.0 - jnp.abs(x_k - x_j) / TILE_X, 0.0
    )
    taper_y = jnp.where(
        (y_k >= oy_j) & (y_k < oy_j + TILE_Y), 1.0 - jnp.abs(y_k - y_j) / TILE_Y, 0.0
    )
    weight = jnp.where(level_j == level_k, 1.0, 0.5) * taper_x * taper_y
    weight = jnp.where(j_ids < k_ids, weight, 0.0)
    pending = jnp.where(weight != 0.0, source, -1.0)
    values = lane_row(value_ref)
    errors = lane_row(error_ref)

    def following(done):
        return jnp.min(jnp.where(pending > done, pending, NONE), axis=0, keepdims=True)

    def step(carry):
        priors, nxt, left = carry
        spread, offset, reduction, factor = innovations(priors, values, errors)
        final = jnp.where(nxt == NONE, 1.0, 0.0)
        table = jnp.concatenate(
            [spread, offset, reduction, factor, final, jnp.zeros((12, total), jnp.float32)], axis=0
        )
        high = table.astype(jnp.bfloat16)
        rest = table - high.astype(jnp.float32)
        middle = rest.astype(jnp.bfloat16)
        low = (rest - middle.astype(jnp.float32)).astype(jnp.bfloat16)
        chosen = source == nxt
        pick = jnp.where(chosen, 1.0, 0.0).astype(jnp.bfloat16)
        dot = lambda part: jnp.dot(part, pick, preferred_element_type=jnp.float32)
        got = dot(high) + dot(middle) + dot(low)
        their_spread = got[:members]
        their_offset, their_reduction, their_factor, ready = (
            got[members + i : members + i + 1] for i in range(4)
        )
        rho = jnp.sum(jnp.where(chosen, weight, 0.0), axis=0, keepdims=True)
        covariance = jnp.sum(priors * their_spread, axis=0, keepdims=True)
        go = ready > 0.5
        scale = jnp.where(go, rho * covariance * their_factor, 0.0)
        priors = priors + scale * (their_offset - their_reduction * their_spread)
        done = jnp.where(go, nxt, nxt - 0.5)
        nxt = following(done)
        return (priors, nxt, jnp.min(nxt))

    nxt = following(jnp.full((1, total), -1.0, jnp.float32))
    priors, _, _ = lax.while_loop(
        lambda carry: carry[2] < NONE, step, (priors, nxt, jnp.min(nxt))
    )
    spread, offset, reduction, factor = innovations(priors, values, errors)
    return (spread * factor, offset - reduction * spread)


def apply_kernel(
    local_members, meta_ref, lanes_ref, value_ref, error_ref, in_ref, *refs
):
    *parts, out_ref, table_ref, work, gain, sems = refs
    members, levels, cols, rows = work.shape
    priors = jnp.concatenate([one[...] for one in parts], axis=0)
    me = lax.axis_index("member")
    table = solve(priors, lanes_ref, value_ref, error_ref)
    for b in range(members // local_members):
        here = pl.ds(pl.multiple_of((b ^ me) * local_members, local_members), local_members)
        for i in range(2):
            table_ref[i, here] = table[i][b * local_members : (b + 1) * local_members]
    part = 8
    base = lax.axis_index("domain") * cols
    row0 = me * rows
    lane = lax.broadcasted_iota(jnp.int32, (1, LANES), 1)
    ox = lanes_ref[3:4]
    oy = lanes_ref[4:5]
    in_rows = (oy < row0 + rows) & (oy + TILE_Y > row0)

    def taper(position, centre, first, span):
        inside = (position >= first) & (position < first + span)
        return jnp.where(inside, 1.0 - jnp.abs(position - centre).astype(jnp.float32) / span, 0.0)

    chunk = members // CHUNKS

    def store(source, n):
        some = pl.ds(n * chunk, chunk)
        return pltpu.make_async_copy(source.at[some], out_ref.at[some], sems.at[n])

    keys = jnp.where(in_rows & (ox < base + cols) & (ox + TILE_X > base), lane, LAST)
    row_ids = row0 + lax.broadcasted_iota(jnp.int32, (part, rows), 1)
    near_ids = base + lax.broadcasted_iota(jnp.int32, (part, rows), 0)
    groups = cols // part
    band = lambda g: pl.ds(g * part, part)
    places = [(l, g) for l in range(levels) for g in range(groups)]

    def ready(k, slot):
        shift = (LANES - k) & 127
        for i in range(2):
            column = pltpu.roll(table_ref[i], shift, 1)[:, 0:1]
            gain[slot, i] = jnp.broadcast_to(column, (members, LANES))

    def update(k, slot, source):
        following = jnp.min(jnp.where(keys > k, keys, LAST))
        along = taper(row_ids, meta_ref[2, k], meta_ref[4, k], TILE_Y)
        weights = [
            taper(near_ids + g * part, meta_ref[1, k], meta_ref[3, k], TILE_X) * along
            for g in range(groups)
        ]
        sums = {}
        for m in range(members):
            s = gain[slot, 0, m : m + 1]
            for l, g in places:
                term = source[m, l, band(g)] * s
                sums[l, g] = sums[l, g] + term if m else term
        scale = {}
        for l, g in places:
            vertical = jnp.where(meta_ref[0, k] == l, 1.0, 0.5)
            scale[l, g] = vertical * weights[g] * sums[l, g]
        ready(following, 1 - slot)
        for m in range(members):
            c = gain[slot, 1, m : m + 1]
            for l, g in places:
                work[m, l, band(g)] = source[m, l, band(g)] + scale[l, g] * c
            if (m + 1) % chunk == 0:

                @pl.when(following == LAST)
                def _(n=m // chunk):
                    store(work, n).start()

        return (following, 1 - slot)

    first = jnp.min(keys)

    @pl.when(first < LAST)
    def _():
        ready(first, 0)
        second = update(first, 0, in_ref)
        lax.while_loop(lambda at: at[0] < LAST, lambda at: update(*at, work), second)

    @pl.when(first == LAST)
    def _():
        for n in range(CHUNKS):
            store(in_ref, n).start()

    for n in range(CHUNKS):
        store(work, n).wait()


def apply_updates(meta, parts, values, errors, block, local_members):
    members, levels, cols, rows = block.shape
    vmem = pl.BlockSpec(memory_space=pltpu.VMEM)
    return pl.pallas_call(
        functools.partial(apply_kernel, local_members),
        out_shape=jax.ShapeDtypeStruct(block.shape, jnp.float32),
        in_specs=[pl.BlockSpec(memory_space=pltpu.SMEM)] + [vmem] * (4 + len(parts)),
        out_specs=pl.BlockSpec(memory_space=pl.ANY),
        scratch_shapes=[
            pltpu.VMEM((2, members, LANES), jnp.float32),
            pltpu.VMEM(block.shape, jnp.float32),
            pltpu.VMEM((2, 2, members, LANES), jnp.float32),
            pltpu.SemaphoreType.DMA((CHUNKS,)),
        ],
        compiler_params=pltpu.CompilerParams(vmem_limit_bytes=VMEM_BYTES),
        name="apply_updates",
    )(*in_hbm(meta), meta, *in_hbm(values, errors), block, *parts)


def exchange(array, axis, peers, reach):
    return lax.ppermute(array, axis, [(i, i ^ reach) for i in range(peers)])


def finish_priors(picked, meta, rates, cols):
    whole, q, u, q_far, u_far = (picked[i] for i in range(PLANES))
    place = meta[1:2] & (cols - 1)
    rate = rates[:, None]
    low = face_flux(u_far, u, q_far, q, rate)
    high = face_flux(u, u_far, q, q_far, rate)
    return whole + jnp.where(place == 0, low, 0.0) - jnp.where(place == cols - 1, high, 0.0)


def local(
    tracer, east_speed, north_speed, diffusivity, obs_cell, tile_offset, obs_value, obs_error
):
    members, levels, cols, length = tracer.shape
    bands = lax.axis_size("member")
    domains = lax.axis_size("domain")
    cells = obs_cell.transpose(2, 0, 1)
    tiles = tile_offset.transpose(0, 2, 1)
    me = lax.axis_index("member")
    rates = jnp.concatenate(
        [lax.dynamic_slice_in_dim(diffusivity, at * members, members) for at in (me, me ^ 1)]
    )
    inner, outer, meta, tracer, east, north = prepare(
        cells, tiles, diffusivity, tracer, east_speed, north_speed, domains
    )
    edges = inner.shape[1] - 8
    got_inner = exchange(inner, "domain", domains, 1)
    picked = inner[:, edges:] + got_inner[:, edges:]
    outer = jnp.concatenate([outer[:, :edges], picked], axis=1)

    def widen(picked, step):
        pairs = [((i + step if i % 2 else i - step) % domains, i) for i in range(domains)]
        return lax.ppermute(picked, "domain", pairs)

    pairs = [(i, (i + 1) % domains if i % 2 else (i - 1) % domains) for i in range(domains)]
    got_outer = lax.ppermute(outer, "domain", pairs)
    far = [widen(picked, step) for step in STEPS]
    tracer, east, north, _ = lax.optimization_barrier((tracer, east, north, outer))
    blocks = interior(diffusivity, tracer, east, north, bands)
    got_outer, far, blocks = lax.optimization_barrier((got_outer, far, blocks))
    picked = (picked + got_outer[:, edges:] + sum(far)).transpose(1, 0, 2)[:PLANES]
    picked = jnp.concatenate([picked, exchange(picked, "member", bands, 1)], axis=1)
    blocks = add_border(diffusivity, inner, outer, got_inner, got_outer, blocks)
    blocks, picked = lax.optimization_barrier((blocks, picked))
    block = lax.all_to_all(blocks, "member", split_axis=0, concat_axis=0, tiled=True)
    block = block.reshape(bands * members, levels, cols, length // bands)
    first = picked
    for step in range(8, domains, 8):
        picked = picked + widen(first, step)
    priors = finish_priors(picked, meta, rates, cols)
    parts = [priors] + [exchange(priors, "member", bands, reach) for reach in range(2, bands, 2)]
    return apply_updates(meta, parts, obs_value, obs_error, block, members)


def solution(mesh):
    placed = (
        P("member", None, "domain", None),
        P("member", "domain", None),
        P("member", "domain", None),
        P(),
        P(),
        P(),
        P(),
        P(),
    )
    return jax.shard_map(
        local,
        mesh=mesh,
        in_specs=placed,
        out_specs=P(None, None, "domain", "member"),
        check_vma=False,
    )
```

```python
import functools

import jax
import jax.numpy as jnp
from jax import lax
from jax.experimental import pallas as pl
from jax.experimental.pallas import tpu as pltpu
from jax.sharding import PartitionSpec as P

TILE_X = 32
TILE_Y = 64
LANES = 128
NONE = 999.0
LAST = 0x7FFFFFFF
PLANES = 5
CHUNKS = 4
STEPS = (4, -2)
VMEM_BYTES = 32 * 1024 * 1024


def lane_row(ref, *index):
    return jnp.concatenate([ref[(*index, slice(0, 1))], ref[(*index, slice(1, 2))]], axis=1)


def copies(pairs, sems):
    made = [pltpu.make_async_copy(src, dst, sems.at[i]) for i, (src, dst) in enumerate(pairs)]
    for one in made:
        one.start()
    return made


def face_flux(u_low, u_high, q_low, q_high, rate):
    face = 0.5 * (u_low + u_high)
    return (
        jnp.maximum(face, 0.0) * q_low + jnp.minimum(face, 0.0) * q_high - rate * (q_high - q_low)
    )


def prepare_kernel(
    domains, cell_hbm, tile_hbm, rate_hbm, tracer_hbm, east_hbm, north_hbm,
    inner_ref, outer_ref, meta_ref, tracer_ref, east_ref, north_ref,
    cell_ref, tile_ref, rate_ref, sems,
):
    members, levels, cols, length = tracer_ref.shape
    bands = length // LANES
    small = copies(
        [(cell_hbm, cell_ref), (tile_hbm, tile_ref), (rate_hbm, rate_ref)], sems.at[0]
    )
    loads = copies(
        [(tracer_hbm, tracer_ref), (east_hbm, east_ref), (north_hbm, north_ref)], sems.at[1]
    )
    for one in small:
        one.wait()
    domain = lax.axis_index("domain")
    me = lax.axis_index("member")
    col0 = domain * cols
    width = domains * cols
    level = lane_row(cell_ref, 0)
    x = lane_row(cell_ref, 1)
    y = lane_row(cell_ref, 2)
    ox = jnp.concatenate([tile_ref[0, 0:1], tile_ref[1, 0:1]], axis=1)
    oy = jnp.concatenate([tile_ref[0, 1:2], tile_ref[1, 1:2]], axis=1)
    lane = lax.broadcasted_iota(jnp.int32, (1, LANES), 1)
    zero = jnp.zeros((3, LANES), jnp.int32)
    meta_ref[...] = jnp.concatenate([level, x, y, ox, oy, zero], axis=0)
    near = (x >= col0) & (x < col0 + cols)
    before = jnp.where(col0 == 0, width, col0) - 1
    after = jnp.where(col0 + cols == width, 0, col0 + cols)
    near = near | (x == before) | (x == after)
    keys = jnp.where(near, (lane << 21) + (level << 19) + (x << 10) + y, LAST)
    for one in loads:
        one.wait()
    first_core = (domain & 1) == 0
    for p in range(levels + 1):
        for d in range(bands):
            at = slice(d * LANES, (d + 1) * LANES)
            plane = tracer_ref.at[:, p] if p < levels else east_ref
            low = plane[:, 0, at]
            high = plane[:, cols - 1, at]
            inner_ref[:, p * bands + d] = jnp.where(first_core, high, low)
            outer_ref[:, p * bands + d] = jnp.where(first_core, low, high)

    sub = lax.broadcasted_iota(jnp.int32, (members, LANES), 0)
    lanes = lax.broadcasted_iota(jnp.int32, (members, LANES), 1)
    rates = jnp.zeros((members, LANES), jnp.float32)
    for m in range(members):
        rates = jnp.where(sub == m, rate_ref[me * members + m], rates)

    def pick(carry):
        key, planes = carry
        following = jnp.min(jnp.where(keys > key, keys, LAST))
        k = key >> 21
        l = (key >> 19) & 3
        col = (key >> 10) & 511
        row = key & 1023
        own = (col >= col0) & (col < col0 + cols)
        here = jnp.where(own, col - col0, jnp.where(col == before, 0, cols - 1))

        def fetch(ref, lead, i, j):
            i = jnp.clip(i, 0, cols - 1)
            j = jnp.clip(j, 0, length - 1)
            first = pl.multiple_of((i >> 3) << 3, 8)
            start = pl.multiple_of((j >> 7) << 7, LANES)
            rows = jnp.zeros((members, LANES), jnp.float32)
            for m in range(members):
                tile = ref[(m, *lead, pl.ds(first, 8), pl.ds(start, LANES))]
                rows = jnp.where(sub == m, pltpu.roll(tile, (m - i) & 7, 0), rows)
            return pltpu.roll(rows, (k - (j & 127) + LANES) & 127, 1)

        q = fetch(tracer_ref, (l,), here, row)
        u = fetch(east_ref, (), here, row)
        v = fetch(north_ref, (), here, row)
        south = face_flux(
            fetch(north_ref, (), here, row - 1), v, fetch(tracer_ref, (l,), here, row - 1), q, rates
        )
        north = face_flux(
            v, fetch(north_ref, (), here, row + 1), q, fetch(tracer_ref, (l,), here, row + 1), rates
        )
        low = face_flux(
            fetch(east_ref, (), here - 1, row), u, fetch(tracer_ref, (l,), here - 1, row), q, rates
        )
        high = face_flux(
            u, fetch(east_ref, (), here + 1, row), q, fetch(tracer_ref, (l,), here + 1, row), rates
        )
        south = jnp.where(row == 0, 0.0, south)
        north = jnp.where(row == length - 1, 0.0, north)
        low = jnp.where(here == 0, 0.0, low)
        high = jnp.where(here == cols - 1, 0.0, high)
        mine = lanes == k
        ours = mine & own
        theirs = mine & jnp.logical_not(own)
        values = (
            (ours, q - (high - low) - (north - south)), (ours, q), (ours, u), (theirs, q), (theirs, u)
        )
        planes = tuple(jnp.where(at, new, old) for (at, new), old in zip(values, planes))
        return (following, planes)

    blank = jnp.zeros((members, LANES), jnp.float32)
    _, planes = lax.while_loop(
        lambda carry: carry[0] < LAST, pick, (jnp.min(keys), (blank,) * PLANES)
    )
    for i, plane in enumerate(planes):
        inner_ref[:, (levels + 1) * bands + i] = plane
    for i in range(PLANES, 8):
        inner_ref[:, (levels + 1) * bands + i] = blank


def in_hbm(*arrays):
    return [pltpu.with_memory_space_constraint(a, pltpu.HBM) for a in arrays]


def prepare(cells, tiles, rates, tracer, east, north, domains):
    members, levels, cols, length = tracer.shape
    vmem = pl.BlockSpec(memory_space=pltpu.VMEM)
    hbm = pl.BlockSpec(memory_space=pltpu.HBM)
    sent = jax.ShapeDtypeStruct(
        (members, (levels + 1) * (length // LANES) + 8, LANES), jnp.float32
    )
    return pl.pallas_call(
        functools.partial(prepare_kernel, domains),
        out_shape=[
            sent,
            sent,
            jax.ShapeDtypeStruct((8, LANES), jnp.int32),
            jax.ShapeDtypeStruct(tracer.shape, jnp.float32),
            jax.ShapeDtypeStruct(east.shape, jnp.float32),
            jax.ShapeDtypeStruct(north.shape, jnp.float32),
        ],
        in_specs=[hbm] * 6,
        out_specs=[vmem] * 6,
        scratch_shapes=[
            pltpu.VMEM(cells.shape, jnp.int32),
            pltpu.VMEM(tiles.shape, jnp.int32),
            pltpu.SMEM(rates.shape, jnp.float32),
            pltpu.SemaphoreType.DMA((2, 3)),
        ],
        compiler_params=pltpu.CompilerParams(vmem_limit_bytes=VMEM_BYTES),
        cost_estimate=pl.CostEstimate(flops=1_000_000, bytes_accessed=3_000_000, transcendentals=0),
        name="prepare",
    )(*in_hbm(cells, tiles, rates, tracer, east, north))


def face_weights(low, high, rate):
    face = 0.5 * (low + high)
    return (jnp.maximum(face, 0.0) + rate, jnp.minimum(face, 0.0) - rate)


def interior_kernel(rate_ref, tracer_ref, east_ref, north_ref, out_ref):
    members, levels, cols, length = tracer_ref.shape
    bands = out_ref.shape[0]
    me = lax.axis_index("member")
    lane = lax.broadcasted_iota(jnp.int32, (cols, LANES), 1)
    none = jnp.zeros((1, LANES), jnp.float32)

    def sides(read, d):
        here = read(d)
        left = jnp.where(lane == LANES - 1, read(d - 1), here) if d else here
        right = jnp.where(lane == 0, read(d + 1), here) if d < bands - 1 else here
        return (pltpu.roll(left, 1, 1), here, pltpu.roll(right, LANES - 1, 1))

    def member(g, carry):
        rate = rate_ref[me * members + g]
        for d in range(bands):
            at = lambda i: pl.ds(i * LANES, LANES)
            u = east_ref[g, :, at(d)]
            behind, ahead = face_weights(u[:-1], u[1:], rate)
            v_left, v, v_right = sides(lambda i: north_ref[g, :, at(i)], d)
            south_low, south_high = face_weights(v_left, v, rate)
            north_low, north_high = face_weights(v, v_right, rate)
            if d == 0:
                south_low = jnp.where(lane == 0, 0.0, south_low)
                south_high = jnp.where(lane == 0, 0.0, south_high)
            if d == bands - 1:
                north_low = jnp.where(lane == LANES - 1, 0.0, north_low)
                north_high = jnp.where(lane == LANES - 1, 0.0, north_high)
            for l in range(levels):
                q_left, q, q_right = sides(lambda i: tracer_ref[g, l, :, at(i)], d)
                flux = behind * q[:-1] + ahead * q[1:]
                flux_low = jnp.concatenate([none, flux], axis=0)
                flux_up = jnp.concatenate([flux, none], axis=0)
                south = south_low * q_left + south_high * q
                north = north_low * q + north_high * q_right
                out_ref[d, g, l] = q - (flux_up - flux_low) - (north - south)
        return carry

    lax.fori_loop(0, members, member, 0)


def interior(rates, tracer, east, north, bands):
    members, levels, cols, length = tracer.shape
    vmem = pl.BlockSpec(memory_space=pltpu.VMEM)
    return pl.pallas_call(
        interior_kernel,
        out_shape=jax.ShapeDtypeStruct((bands, members, levels, cols, LANES), jnp.float32),
        in_specs=[pl.BlockSpec(memory_space=pltpu.SMEM)] + [vmem] * 3,
        out_specs=vmem,
        compiler_params=pltpu.CompilerParams(vmem_limit_bytes=VMEM_BYTES),
        cost_estimate=pl.CostEstimate(
            flops=16_000_000, bytes_accessed=4_500_000, transcendentals=0
        ),
        name="interior",
    )(*in_hbm(rates), tracer, east, north)


def border_kernel(
    rate_ref, inner_ref, outer_ref, got_inner_ref, got_outer_ref, in_ref, out_any, out_ref, sems
):
    bands, members, levels, cols, lanes = in_ref.shape
    store = lambda g: pltpu.make_async_copy(out_ref.at[:, g], out_any.at[:, g], sems.at[g])
    me = lax.axis_index("member")
    first_core = (lax.axis_index("domain") & 1) == 0
    row = lax.broadcasted_iota(jnp.int32, (8, lanes), 0)

    def member(g, carry):
        rate = rate_ref[me * members + g]

        def plane(p):
            at = pl.ds(p * bands, bands)
            inner, outer = inner_ref[g, at], outer_ref[g, at]
            got_inner, got_outer = got_inner_ref[g, at], got_outer_ref[g, at]
            return (
                jnp.where(first_core, got_outer, got_inner),
                jnp.where(first_core, outer, inner),
                jnp.where(first_core, inner, outer),
                jnp.where(first_core, got_inner, got_outer),
            )

        u_below, u_first, u_last, u_above = plane(levels)
        enter = face_weights(u_below, u_first, rate)
        leave = face_weights(u_last, u_above, rate)
        for l in range(levels):
            below, first, last, above = plane(l)
            low = enter[0] * below + enter[1] * first
            high = leave[0] * last + leave[1] * above
            for d in range(bands):
                top = jnp.where(row == 0, pltpu.roll(low, (8 - d) % 8, 0), 0.0)
                bottom = jnp.where(row == 7, pltpu.roll(high, 7 - d, 0), 0.0)
                out_ref[d, g, l, :8] = in_ref[d, g, l, :8] + top
                if cols > 16:
                    out_ref[d, g, l, 8 : cols - 8] = in_ref[d, g, l, 8 : cols - 8]
                out_ref[d, g, l, cols - 8 :] = in_ref[d, g, l, cols - 8 :] - bottom
        store(g).start()
        return carry

    lax.fori_loop(0, members, member, 0, unroll=4)
    for g in range(members):
        store(g).wait()


def add_border(rates, inner, outer, got_inner, got_outer, blocks):
    vmem = pl.BlockSpec(memory_space=pltpu.VMEM)
    return pl.pallas_call(
        border_kernel,
        out_shape=jax.ShapeDtypeStruct(blocks.shape, jnp.float32),
        in_specs=[pl.BlockSpec(memory_space=pltpu.SMEM)] + [vmem] * 5,
        out_specs=pl.BlockSpec(memory_space=pl.ANY),
        scratch_shapes=[
            pltpu.VMEM(blocks.shape, jnp.float32),
            pltpu.SemaphoreType.DMA((blocks.shape[1],)),
        ],
        compiler_params=pltpu.CompilerParams(vmem_limit_bytes=VMEM_BYTES),
        cost_estimate=pl.CostEstimate(flops=1_000_000, bytes_accessed=3_000_000, transcendentals=0),
        name="add_border",
    )(*in_hbm(rates), inner, outer, got_inner, got_outer, blocks)


def innovations(priors, values, errors):
    members = priors.shape[0]
    average = jnp.sum(priors, axis=0, keepdims=True) / members
    spread = priors - average
    variance = jnp.sum(spread * spread, axis=0, keepdims=True) / (members - 1)
    divisor = variance + errors
    reduction = 1.0 / (1.0 + jnp.sqrt(errors / divisor))
    factor = 1.0 / ((members - 1) * divisor)
    return (spread, values - average, reduction, factor)


def solve(priors, meta_ref, value_ref, error_ref):
    members, total = priors.shape
    meta = meta_ref[...].astype(jnp.float32)
    across = jnp.concatenate(
        [meta, jnp.zeros((total - meta.shape[0], total), jnp.float32)], axis=0
    ).T
    level_j, x_j, y_j, ox_j, oy_j = (across[:, i : i + 1] for i in range(5))
    level_k, x_k, y_k = (meta[i : i + 1] for i in range(3))
    j_ids = lax.broadcasted_iota(jnp.int32, (total, total), 0)
    k_ids = lax.broadcasted_iota(jnp.int32, (total, total), 1)
    source = j_ids.astype(jnp.float32)
    taper_x = jnp.where(
        (x_k >= ox_j) & (x_k < ox_j + TILE_X), 1.0 - jnp.abs(x_k - x_j) / TILE_X, 0.0
    )
    taper_y = jnp.where(
        (y_k >= oy_j) & (y_k < oy_j + TILE_Y), 1.0 - jnp.abs(y_k - y_j) / TILE_Y, 0.0
    )
    weight = jnp.where(level_j == level_k, 1.0, 0.5) * taper_x * taper_y
    weight = jnp.where(j_ids < k_ids, weight, 0.0)
    pending = jnp.where(weight != 0.0, source, -1.0)
    values = lane_row(value_ref)
    errors = lane_row(error_ref)

    def following(done):
        return jnp.min(jnp.where(pending > done, pending, NONE), axis=0, keepdims=True)

    def step(carry):
        priors, nxt, left = carry
        spread, offset, reduction, factor = innovations(priors, values, errors)
        final = jnp.where(nxt == NONE, 1.0, 0.0)
        table = jnp.concatenate(
            [spread, offset, reduction, factor, final, jnp.zeros((12, total), jnp.float32)], axis=0
        )
        high = table.astype(jnp.bfloat16)
        rest = table - high.astype(jnp.float32)
        middle = rest.astype(jnp.bfloat16)
        low = (rest - middle.astype(jnp.float32)).astype(jnp.bfloat16)
        chosen = source == nxt
        pick = jnp.where(chosen, 1.0, 0.0).astype(jnp.bfloat16)
        pieces = jnp.concatenate([high, middle, low], axis=0)
        found = jnp.dot(pieces, pick, preferred_element_type=jnp.float32)
        size = table.shape[0]
        got = found[:size] + found[size : 2 * size] + found[2 * size :]
        their_spread = got[:members]
        their_offset, their_reduction, their_factor, ready = (
            got[members + i : members + i + 1] for i in range(4)
        )
        rho = jnp.sum(jnp.where(chosen, weight, 0.0), axis=0, keepdims=True)
        covariance = jnp.sum(priors * their_spread, axis=0, keepdims=True)
        go = ready > 0.5
        scale = jnp.where(go, rho * covariance * their_factor, 0.0)
        priors = priors + scale * (their_offset - their_reduction * their_spread)
        done = jnp.where(go, nxt, nxt - 0.5)
        nxt = following(done)
        return (priors, nxt, jnp.min(nxt))

    nxt = following(jnp.full((1, total), -1.0, jnp.float32))
    priors, _, _ = lax.while_loop(
        lambda carry: carry[2] < NONE, step, (priors, nxt, jnp.min(nxt))
    )
    spread, offset, reduction, factor = innovations(priors, values, errors)
    return (spread * factor, offset - reduction * spread)


def apply_kernel(
    local_members, meta_ref, lanes_ref, value_ref, error_ref, in_ref, *refs
):
    *parts, out_ref, table_ref, work, gain, sems = refs
    members, levels, cols, rows = work.shape
    priors = jnp.concatenate([one[...] for one in parts], axis=0)
    me = lax.axis_index("member")
    table = solve(priors, lanes_ref, value_ref, error_ref)
    for b in range(members // local_members):
        here = pl.ds(pl.multiple_of((b ^ me) * local_members, local_members), local_members)
        for i in range(2):
            table_ref[i, here] = table[i][b * local_members : (b + 1) * local_members]
    part = 8
    base = lax.axis_index("domain") * cols
    row0 = me * rows
    lane = lax.broadcasted_iota(jnp.int32, (1, LANES), 1)
    ox = lanes_ref[3:4]
    oy = lanes_ref[4:5]
    in_rows = (oy < row0 + rows) & (oy + TILE_Y > row0)

    def taper(position, centre, first, span):
        inside = (position >= first) & (position < first + span)
        return jnp.where(inside, 1.0 - jnp.abs(position - centre).astype(jnp.float32) / span, 0.0)

    chunk = members // CHUNKS

    def store(source, n):
        some = pl.ds(n * chunk, chunk)
        return pltpu.make_async_copy(source.at[some], out_ref.at[some], sems.at[n])

    keys = jnp.where(in_rows & (ox < base + cols) & (ox + TILE_X > base), lane, LAST)
    row_ids = row0 + lax.broadcasted_iota(jnp.int32, (part, rows), 1)
    near_ids = base + lax.broadcasted_iota(jnp.int32, (part, rows), 0)
    groups = cols // part
    band = lambda g: pl.ds(g * part, part)
    places = [(l, g) for l in range(levels) for g in range(groups)]

    def ready(k, slot):
        shift = (LANES - k) & 127
        for i in range(2):
            column = pltpu.roll(table_ref[i], shift, 1)[:, 0:1]
            gain[slot, i] = jnp.broadcast_to(column, (members, LANES))

    def update(k, slot, source):
        following = jnp.min(jnp.where(keys > k, keys, LAST))
        along = taper(row_ids, meta_ref[2, k], meta_ref[4, k], TILE_Y)
        weights = [
            taper(near_ids + g * part, meta_ref[1, k], meta_ref[3, k], TILE_X) * along
            for g in range(groups)
        ]
        sums = {}
        for m in range(members):
            s = gain[slot, 0, m : m + 1]
            for l, g in places:
                term = source[m, l, band(g)] * s
                sums[l, g] = sums[l, g] + term if m else term
        scale = {}
        for l, g in places:
            vertical = jnp.where(meta_ref[0, k] == l, 1.0, 0.5)
            scale[l, g] = vertical * weights[g] * sums[l, g]
        ready(following, 1 - slot)
        for m in range(members):
            c = gain[slot, 1, m : m + 1]
            for l, g in places:
                work[m, l, band(g)] = source[m, l, band(g)] + scale[l, g] * c
            if (m + 1) % chunk == 0:

                @pl.when(following == LAST)
                def _(n=m // chunk):
                    store(work, n).start()

        return (following, 1 - slot)

    first = jnp.min(keys)

    @pl.when(first < LAST)
    def _():
        ready(first, 0)
        second = update(first, 0, in_ref)
        lax.while_loop(lambda at: at[0] < LAST, lambda at: update(*at, work), second)

    @pl.when(first == LAST)
    def _():
        for n in range(CHUNKS):
            store(in_ref, n).start()

    for n in range(CHUNKS):
        store(work, n).wait()


def apply_updates(meta, parts, values, errors, block, local_members):
    members, levels, cols, rows = block.shape
    vmem = pl.BlockSpec(memory_space=pltpu.VMEM)
    return pl.pallas_call(
        functools.partial(apply_kernel, local_members),
        out_shape=jax.ShapeDtypeStruct(block.shape, jnp.float32),
        in_specs=[pl.BlockSpec(memory_space=pltpu.SMEM)] + [vmem] * (4 + len(parts)),
        out_specs=pl.BlockSpec(memory_space=pl.ANY),
        scratch_shapes=[
            pltpu.VMEM((2, members, LANES), jnp.float32),
            pltpu.VMEM(block.shape, jnp.float32),
            pltpu.VMEM((2, 2, members, LANES), jnp.float32),
            pltpu.SemaphoreType.DMA((CHUNKS,)),
        ],
        compiler_params=pltpu.CompilerParams(vmem_limit_bytes=VMEM_BYTES),
        name="apply_updates",
    )(*in_hbm(meta), meta, *in_hbm(values, errors), block, *parts)


def exchange(array, axis, peers, reach):
    return lax.ppermute(array, axis, [(i, i ^ reach) for i in range(peers)])


def finish_priors(picked, meta, rates, cols):
    whole, q, u, q_far, u_far = (picked[i] for i in range(PLANES))
    place = meta[1:2] & (cols - 1)
    rate = rates[:, None]
    low = face_flux(u_far, u, q_far, q, rate)
    high = face_flux(u, u_far, q, q_far, rate)
    return whole + jnp.where(place == 0, low, 0.0) - jnp.where(place == cols - 1, high, 0.0)


def local(
    tracer, east_speed, north_speed, diffusivity, obs_cell, tile_offset, obs_value, obs_error
):
    members, levels, cols, length = tracer.shape
    bands = lax.axis_size("member")
    domains = lax.axis_size("domain")
    cells = obs_cell.transpose(2, 0, 1)
    tiles = tile_offset.transpose(0, 2, 1)
    me = lax.axis_index("member")
    rates = jnp.concatenate(
        [lax.dynamic_slice_in_dim(diffusivity, at * members, members) for at in (me, me ^ 1)]
    )
    inner, outer, meta, tracer, east, north = prepare(
        cells, tiles, diffusivity, tracer, east_speed, north_speed, domains
    )
    edges = inner.shape[1] - 8
    got_inner = exchange(inner, "domain", domains, 1)
    picked = inner[:, edges:] + got_inner[:, edges:]
    outer = jnp.concatenate([outer[:, :edges], picked], axis=1)

    def widen(picked, step):
        pairs = [((i + step if i % 2 else i - step) % domains, i) for i in range(domains)]
        return lax.ppermute(picked, "domain", pairs)

    pairs = [(i, (i + 1) % domains if i % 2 else (i - 1) % domains) for i in range(domains)]
    got_outer = lax.ppermute(outer, "domain", pairs)
    far = [widen(picked, step) for step in STEPS]
    tracer, east, north, _ = lax.optimization_barrier((tracer, east, north, outer))
    blocks = interior(diffusivity, tracer, east, north, bands)
    got_outer, far, blocks = lax.optimization_barrier((got_outer, far, blocks))
    picked = (picked + got_outer[:, edges:] + sum(far)).transpose(1, 0, 2)[:PLANES]
    picked = jnp.concatenate([picked, exchange(picked, "member", bands, 1)], axis=1)
    blocks = add_border(diffusivity, inner, outer, got_inner, got_outer, blocks)
    blocks, picked = lax.optimization_barrier((blocks, picked))
    block = lax.all_to_all(blocks, "member", split_axis=0, concat_axis=0, tiled=True)
    block = block.reshape(bands * members, levels, cols, length // bands)
    first = picked
    for step in range(8, domains, 8):
        picked = picked + widen(first, step)
    priors = finish_priors(picked, meta, rates, cols)
    parts = [priors] + [exchange(priors, "member", bands, reach) for reach in range(2, bands, 2)]
    return apply_updates(meta, parts, obs_value, obs_error, block, members)


def solution(mesh):
    placed = (
        P("member", None, "domain", None),
        P("member", "domain", None),
        P("member", "domain", None),
        P(),
        P(),
        P(),
        P(),
        P(),
    )
    return jax.shard_map(
        local,
        mesh=mesh,
        in_specs=placed,
        out_specs=P(None, None, "domain", "member"),
        check_vma=False,
    )
```
